32 devices in a mesh: row: 4 (over z), col: 8 (over y, x, core).
Axes of the slice: x: 2, y: 2, z: 4, core: 2. Of those that a mesh axis runs over, the one named last changes fastest.
Arguments:
- blocks: bfloat16 [4, 8, 256, 128, 128], P('row', 'col'), may hold values from 0 to 0.0625
- slot_rows: int32 [4, 8, 256], P('row', 'col'), may hold values from 0 to 63, as said below
- slot_cols: int32 [4, 8, 256], P('row', 'col'), may hold values from 0 to 31, as said below
- counts: int32 [4, 8], P('row', 'col'), may hold values from 0 to 256, as said below
- reward_table: bfloat16 [32, 32768], P('row', 'col'), may hold values from -6 to 6
- reward_cols: int32 [16], replicated, may hold values from 0 to 31, as said below
- cotangent: bfloat16 [16, 32768], P(None, ('row', 'col')), may hold values from -6 to 6
Outputs:
- value: float32 [16, 32768], P(None, ('row', 'col'))
- grad: float32 [16, 32768], P('row', 'col')
The draws below stay inside these ranges and needn't reach their ends.
Inputs may be any that keep to these rules, and one draw needn't show every extreme that they name: `counts`: stored blocks of each grid cell; along every grid row the cells of even index hold 512 of them, and so do the cells of odd index, and some cell of every grid row holds exactly 256. Only the first counts[a, b] slots of a grid cell hold stored blocks; every block row has exactly 16 stored blocks; slot_rows[a, b, s] is even where b is even and odd where b is odd. `slot_cols`: two stored blocks at the same position add. `reward_cols`: distinct candidates.
All inputs are finite; a program needn't handle non-finite values.
Results may differ from the reference program's by a relative error of at most 0.0003.
Values may be sent and summed in bfloat16 or wider, within the bound.
No kernel may reach another device: no remote copies, remote signals or barrier semaphores. Data moves between devices by JAX's collectives and lax.ppermute only.
A program may use at most 64 MiB of HBM per device.

```python
import jax
import jax.numpy as jnp
from jax import lax

BLK = 128
REWARDS = 16
CANDIDATES = 32
MEAN_DEV = 128
CAP = 256
SB_ROW = 64
SB_COL = 32
STATES = 32768
N_ROW = 4
N_COL = 8


def pattern(key):
    folded = jax.random.fold_in(key, 7001)
    subkeys = jax.random.split(folded, 4)
    half_cols = N_COL // 2
    quarter_cols = N_COL // 4
    half_rows = SB_ROW // 2
    swings = jax.random.randint(subkeys[0], (N_ROW, 2, quarter_cols), 0, MEAN_DEV + 1)
    swings = swings.at[:, :, 0].set(MEAN_DEV)
    paired = jnp.concatenate([MEAN_DEV + swings, MEAN_DEV - swings], axis=2)
    shuffle_keys = jax.random.split(subkeys[1], N_ROW * 2)
    shuffles = jax.vmap(lambda subkey: jax.random.permutation(subkey, half_cols))(shuffle_keys).reshape(N_ROW, 2, half_cols)
    grouped = jnp.take_along_axis(paired, shuffles, axis=2).astype(jnp.int32)
    starts = jnp.cumsum(grouped, axis=2) - grouped
    counts = jnp.transpose(grouped, (0, 2, 1)).reshape(N_ROW, N_COL)
    offsets = jnp.transpose(starts, (0, 2, 1)).reshape(N_ROW, N_COL)
    order_keys = jax.random.split(subkeys[2], N_ROW * 2)
    row_order = jax.vmap(lambda subkey: jax.random.permutation(subkey, half_rows))(order_keys).reshape(N_ROW, 2, half_rows)
    parity = jnp.arange(N_COL, dtype=jnp.int32) % 2
    cell_order = row_order[:, parity, :]
    serial = (offsets[:, :, None] + jnp.arange(CAP, dtype=jnp.int32)[None, None, :]) % half_rows
    pairs_index = jnp.take_along_axis(cell_order, serial, axis=2)
    slot_row_ids = 2 * pairs_index + parity[None, :, None]
    slot_col_ids = jax.random.randint(subkeys[3], (N_ROW, N_COL, CAP), 0, SB_COL)
    return (counts, slot_row_ids.astype(jnp.int32), slot_col_ids.astype(jnp.int32))


def draw_counts(key, part):
    return pattern(key)[0]


def draw_slot_rows(key, part):
    return pattern(key)[1]


def draw_slot_cols(key, part):
    return pattern(key)[2]


def draw_reward_cols(key, part):
    chosen = jax.random.permutation(jax.random.fold_in(key, 7003), CANDIDATES)
    return chosen[:REWARDS].astype(jnp.int32)


def block_scale(own_key, extent, shards, low, top_value):
    factor_of, own = 1.0, jax.random.fold_in(own_key, 6)
    for axis_at, parts in shards:
        heights = jnp.exp(jax.random.uniform(jax.random.fold_in(own, axis_at), (parts,), jnp.float32, low / len(shards), top_value / len(shards)))
        factor_of = factor_of * jnp.repeat(heights, extent[axis_at] // parts).reshape([-1 if axis == axis_at else 1 for axis in range(len(extent))])
    return factor_of


def noise(key, extent, width, most, cuts=(), kind=jnp.bfloat16):
    values = width * jax.random.normal(key, extent, jnp.float32)
    if cuts:
        values = values * block_scale(key, extent, cuts, -0.22, 0.18)
    return jnp.clip(values, -most, most).astype(kind)


def setup_inputs(seed: int = 0) -> dict:
    splits = jax.random.split(jax.random.key(seed), 8)
    blocks = jnp.clip(0.0625 * jax.random.uniform(splits[0], (N_ROW, N_COL, CAP, BLK, BLK), jnp.float32) ** block_scale(splits[0], (N_ROW, N_COL, CAP, BLK, BLK), ((0, 4), (1, 8)), -0.2, 0.2), 0.0, 0.0625).astype(jnp.bfloat16)
    slot_rows = draw_slot_rows(jax.random.fold_in(splits[7], 71), 0)
    slot_cols = draw_slot_cols(jax.random.fold_in(splits[7], 71), 0)
    counts = draw_counts(jax.random.fold_in(splits[7], 71), 0)
    reward_table = noise(splits[4], (CANDIDATES, STATES), 1.0, 6.0, ((0, 4), (1, 8)))
    reward_cols = draw_reward_cols(jax.random.fold_in(splits[7], 71), 0)
    cotangent = noise(splits[6], (REWARDS, STATES), 1.0, 6.0, ((1, 32),))
    return {"blocks": blocks, "slot_rows": slot_rows, "slot_cols": slot_cols, "counts": counts, "reward_table": reward_table, "reward_cols": reward_cols, "cotangent": cotangent}


def reference(blocks, slot_rows, slot_cols, counts, reward_table, reward_cols, cotangent):
    rewards = jnp.take(reward_table, reward_cols, axis=0)
    reward_cells = rewards.reshape(REWARDS, N_COL, SB_COL, BLK).astype(jnp.float32)
    weight_cells = cotangent.reshape(REWARDS, N_ROW, SB_ROW, BLK).astype(jnp.float32)
    slot_index = jnp.arange(CAP, dtype=jnp.int32)

    def visit(totals, cell_index):
        value_acc, grad_acc = totals
        grid_row = cell_index // N_COL
        grid_col = cell_index % N_COL
        stored = blocks[grid_row, grid_col].astype(jnp.float32)
        rows_here = slot_rows[grid_row, grid_col]
        cols_here = slot_cols[grid_row, grid_col]
        live_mask = (slot_index < counts[grid_row, grid_col]).astype(jnp.float32)[None, :, None]
        picked = jnp.take(reward_cells[:, grid_col], cols_here, axis=1)
        forward = jnp.einsum("kgc,grc->kgr", picked, stored) * live_mask
        value_acc = value_acc.at[:, grid_row, rows_here].add(forward)
        weights = jnp.take(weight_cells[:, grid_row], rows_here, axis=1)
        backward = jnp.einsum("kgr,grc->kgc", weights, stored) * live_mask
        grad_acc = grad_acc.at[:, grid_col, cols_here].add(backward)
        return (value_acc, grad_acc), None

    start_values = jnp.zeros((REWARDS, N_ROW, SB_ROW, BLK), jnp.float32)
    start_grads = jnp.zeros((REWARDS, N_COL, SB_COL, BLK), jnp.float32)
    cells = jnp.arange(N_ROW * N_COL, dtype=jnp.int32)
    (value_acc, grad_acc), _ = lax.scan(visit, (start_values, start_grads), cells)
    return value_acc.reshape(REWARDS, STATES), grad_acc.reshape(REWARDS, STATES)
```

```python
import functools

import jax
import jax.numpy as jnp
from jax import lax
from jax.experimental import pallas as pl
from jax.experimental.pallas import tpu as pltpu
from jax.sharding import PartitionSpec as P

BLK = 128
REWARDS = 16
CHUNK = 64
VMEM_LIMIT = 40 * 2**20


def peers(size, step):
    return [(here, here ^ step) for here in range(size)]


def tile_of(blocks, slots):
    stored = [blocks[0, 0, slot] for slot in slots]
    left = jnp.concatenate(stored[:2], axis=0)
    right = jnp.concatenate(stored[2:], axis=0)
    return jnp.concatenate([left, right], axis=1)


def spread(first, second):
    empty = jnp.zeros((2 * REWARDS, BLK), jnp.bfloat16)
    top = jnp.concatenate([jnp.concatenate(first, axis=0), empty], axis=1)
    bottom = jnp.concatenate([empty, jnp.concatenate(second, axis=0)], axis=1)
    return jnp.concatenate([top, bottom], axis=0)


def each_chunk(live_count, visit):
    chunks = (live_count + CHUNK - 1) // CHUNK
    lax.fori_loop(0, chunks, lambda chunk, carry: (visit(chunk * CHUNK), carry)[1], 0)


def places(slot, live_count, slot_rows, slot_cols, row_cells, col_cells):
    live = slot < live_count
    row = jnp.where(live, slot_rows[0, 0, slot] // 2, row_cells)
    col = jnp.where(live, slot_cols[0, 0, slot], col_cells)
    return row, col


def adjoint_kernel(n_row, n_col, slot_rows, slot_cols, counts, blocks, *refs):
    shards, sends = refs[:n_col], refs[n_col : n_col + n_row]
    weights, totals = refs[n_col + n_row :]
    own_row, own_col = lax.axis_index("row"), lax.axis_index("col")
    row_cells, col_cells = weights.shape[0] - 1, totals.shape[0] - 1
    owned = row_cells // n_col
    parity = own_col % 2
    for step, shard in enumerate(shards):
        first = (own_col ^ step) * owned
        for at in range(owned):
            lane = pl.multiple_of((2 * at + parity) * BLK, BLK)
            weights[first + at] = shard[:, pl.ds(lane, BLK)]
    weights[row_cells] = jnp.zeros((REWARDS, BLK), jnp.bfloat16)
    totals[...] = jnp.zeros_like(totals)
    live_count = counts[0, 0]

    def visit(start):
        found = []
        for quad in range(0, CHUNK, 4):
            slots = [start + quad + at for at in range(4)]
            at = [places(s, live_count, slot_rows, slot_cols, row_cells, col_cells) for s in slots]
            factor = [weights[row] for row, _ in at]
            product = lax.dot_general(
                spread((factor[0], factor[2]), (factor[1], factor[3])),
                tile_of(blocks, slots),
                (((1,), (0,)), ((), ())),
                preferred_element_type=jnp.float32,
            )
            for piece, (which, side) in enumerate(((0, 0), (2, 1), (1, 0), (3, 1))):
                found.append(
                    (
                        at[which][1],
                        product[piece * REWARDS : (piece + 1) * REWARDS, side * BLK : (side + 1) * BLK],
                    )
                )
        for col, part in found:
            totals[col] += part

    each_chunk(live_count, visit)
    group = REWARDS // n_row
    for step, send in enumerate(sends):
        first = (own_row ^ step) * group
        for col in range(col_cells):
            send[:, col * BLK : (col + 1) * BLK] = totals[col, pl.ds(first, group), :]


def forward_kernel(n_row, n_col, slot_rows, slot_cols, counts, reward_cols, blocks, *refs):
    n_chip = n_col // 2
    tables, sends = refs[:n_row], refs[n_row : n_row + n_chip]
    table, rewards, totals = refs[n_row + n_chip :]
    own_row, own_chip = lax.axis_index("row"), lax.axis_index("col") // 2
    row_cells, col_cells = totals.shape[0] - 1, rewards.shape[0] - 1
    group = tables[0].shape[0]
    candidates = group * n_row
    for step, part in enumerate(tables):
        table[step * group : (step + 1) * group, :] = part[...].astype(jnp.float32)
    lane = lax.broadcasted_iota(jnp.int32, (REWARDS, candidates), 1)
    column = lane % group + (own_row ^ (lane // group)) * group
    line = lax.broadcasted_iota(jnp.int32, (REWARDS, candidates), 0)
    wanted = jnp.zeros((REWARDS, candidates), jnp.int32)
    for k in range(REWARDS):
        wanted = jnp.where(line == k, reward_cols[k], wanted)
    pick = (column == wanted).astype(jnp.float32).astype(jnp.bfloat16)
    for col in range(col_cells):
        rewards[col] = jnp.dot(
            pick,
            table[:, col * BLK : (col + 1) * BLK].astype(jnp.bfloat16),
            preferred_element_type=jnp.float32,
        ).astype(jnp.bfloat16)
    rewards[col_cells] = jnp.zeros((REWARDS, BLK), jnp.bfloat16)
    totals[...] = jnp.zeros_like(totals)
    live_count = counts[0, 0]

    def visit(start):
        found = []
        for quad in range(0, CHUNK, 4):
            slots = [start + quad + at for at in range(4)]
            at = [places(s, live_count, slot_rows, slot_cols, row_cells, col_cells) for s in slots]
            factor = [rewards[col] for _, col in at]
            product = lax.dot_general(
                spread((factor[0], factor[1]), (factor[2], factor[3])),
                tile_of(blocks, slots),
                (((1,), (1,)), ((), ())),
                preferred_element_type=jnp.float32,
            )
            for piece, (which, side) in enumerate(((0, 0), (1, 1), (2, 0), (3, 1))):
                found.append(
                    (
                        at[which][0],
                        product[piece * REWARDS : (piece + 1) * REWARDS, side * BLK : (side + 1) * BLK],
                    )
                )
        for row, part in found:
            totals[row] += part

    each_chunk(live_count, visit)
    part = row_cells // n_chip
    for step, send in enumerate(sends):
        send[...] = totals[pl.ds((own_chip ^ step) * part, part)]


def join_kernel(own, other, out):
    parity = lax.axis_index("col") % 2
    part = own.shape[0] // 2
    for at in range(part):
        here, there = own[parity * part + at], other[parity * part + at]
        even = jnp.where(parity == 0, here, there)
        odd = jnp.where(parity == 0, there, here)
        out[:, 2 * at * BLK : (2 * at + 1) * BLK] = even
        out[:, (2 * at + 1) * BLK : (2 * at + 2) * BLK] = odd


def on_device(n_row, n_col, blocks, slot_rows, slot_cols, counts, reward_table, reward_cols, cotangent):
    n_chip = n_col // 2
    row_cells = n_col * (cotangent.shape[1] // BLK) // 2
    col_cells = reward_table.shape[1] // BLK
    smem = pl.BlockSpec(memory_space=pltpu.SMEM)
    vmem = pl.BlockSpec(memory_space=pltpu.VMEM)
    params = pltpu.CompilerParams(vmem_limit_bytes=VMEM_LIMIT)

    tables = [reward_table] + [
        lax.ppermute(reward_table, "row", peers(n_row, step)) for step in range(1, n_row)
    ]
    shards = []
    for chip in range(n_chip):
        here = lax.ppermute(cotangent, "col", peers(n_col, 2 * chip)) if chip else cotangent
        shards += [here, lax.ppermute(here, "col", peers(n_col, 1))]

    group = REWARDS // n_row
    grads = pl.pallas_call(
        functools.partial(adjoint_kernel, n_row, n_col),
        out_shape=[jax.ShapeDtypeStruct((group, col_cells * BLK), jnp.float32)] * n_row,
        in_specs=[smem] * 3 + [vmem] * (1 + n_col),
        out_specs=[vmem] * n_row,
        scratch_shapes=[
            pltpu.VMEM((row_cells + 1, REWARDS, BLK), jnp.bfloat16),
            pltpu.VMEM((col_cells + 1, REWARDS, BLK), jnp.float32),
        ],
        compiler_params=params,
    )(slot_rows, slot_cols, counts, blocks, *shards)
    grad = grads[0]
    for step in range(1, n_row):
        grad = grad + lax.ppermute(grads[step], "row", peers(n_row, step))

    part = row_cells // n_chip
    values = pl.pallas_call(
        functools.partial(forward_kernel, n_row, n_col),
        out_shape=[jax.ShapeDtypeStruct((part, REWARDS, BLK), jnp.float32)] * n_chip,
        in_specs=[smem] * 4 + [vmem] * (1 + n_row),
        out_specs=[vmem] * n_chip,
        scratch_shapes=[
            pltpu.VMEM((reward_table.shape[0] * n_row, col_cells * BLK), jnp.float32),
            pltpu.VMEM((col_cells + 1, REWARDS, BLK), jnp.bfloat16),
            pltpu.VMEM((row_cells + 1, REWARDS, BLK), jnp.float32),
        ],
        compiler_params=params,
    )(slot_rows, slot_cols, counts, reward_cols, blocks, *tables)
    value = values[0]
    for step in range(1, n_chip):
        value = value + lax.ppermute(values[step], "col", peers(n_col, 2 * step))
    other = lax.ppermute(value, "col", peers(n_col, 1))
    value = pl.pallas_call(
        join_kernel,
        out_shape=jax.ShapeDtypeStruct((REWARDS, part * BLK), jnp.float32),
        in_specs=[vmem, vmem],
        out_specs=vmem,
    )(value, other)
    return value, grad


def solution(mesh):
    placed = (
        P("row", "col", None, None, None),
        P("row", "col", None),
        P("row", "col", None),
        P("row", "col"),
        P("row", "col"),
        P(),
        P(None, ("row", "col")),
    )
    return jax.shard_map(
        functools.partial(on_device, mesh.shape["row"], mesh.shape["col"]),
        mesh=mesh,
        in_specs=placed,
        out_specs=(P(None, ("row", "col")), P("row", "col")),
        check_vma=False,
    )
```

```python
import functools

import jax
import jax.numpy as jnp
from jax import lax
from jax.experimental import pallas as pl
from jax.experimental.pallas import tpu as pltpu
from jax.sharding import PartitionSpec as P

BLK = 128
REWARDS = 16
CHUNK = 64
SUMS = 4
VMEM_LIMIT = 40 * 2**20


def peers(size, step):
    return [(here, here ^ step) for here in range(size)]


def crossings(n_row, n_col, step):
    pairs = []
    for row in range(n_row):
        for chip in range(n_col // 2):
            if step < n_col // 2:
                pairs.append((row * n_col + 2 * chip, row * n_col + 2 * (chip ^ step)))
            if step < n_row:
                pairs.append((row * n_col + 2 * chip + 1, (row ^ step) * n_col + 2 * chip + 1))
    return pairs


def by_core(here, there):
    first = lax.axis_index("col") % 2 == 0
    return jnp.where(first, here, there), jnp.where(first, there, here)


def lay(table, width):
    pieces = table.shape[1] // width
    return jnp.concatenate([table[:, at * width : (at + 1) * width] for at in range(pieces)], axis=0)


def gather_kernel(shard_there, table_there, other_shard, other_table, out, shard, table, sems):
    copies = [
        pltpu.make_async_copy(shard_there, shard, sems.at[0]),
        pltpu.make_async_copy(table_there, table, sems.at[1]),
    ]
    for copy in copies:
        copy.start()
    for copy in copies:
        copy.wait()
    core, span, width = lax.axis_index("col") % 2, shard.shape[1], out.shape[1]

    @pl.when(core == 0)
    def _():
        out[:, :span] = shard[...]
        out[:, span : 2 * span] = other_shard[...]

    @pl.when(core == 1)
    def _():
        lines = [lay(part[...].astype(jnp.float32), width) for part in (other_table, table)]
        out[...] = jnp.concatenate(lines, axis=0).astype(out.dtype)


def spread(first, second):
    empty = jnp.zeros((2 * REWARDS, BLK), jnp.bfloat16)
    top = jnp.concatenate([jnp.concatenate(first, axis=0), empty], axis=1)
    bottom = jnp.concatenate([empty, jnp.concatenate(second, axis=0)], axis=1)
    return jnp.concatenate([top, bottom], axis=0)


def products_kernel(n_row, n_col, *refs):
    n_chip = n_col // 2
    steps = max(n_row, n_chip)
    counts, slot_rows_there, slot_cols_there, reward_cols_there, blocks_there = refs[:5]
    mine, others = refs[5 : 5 + steps], refs[5 + steps : 5 + 2 * steps]
    keeps, gives = refs[5 + 2 * steps : 5 + 3 * steps], refs[5 + 3 * steps : 5 + 4 * steps]
    refs = refs[5 + 4 * steps :]
    slot_rows, slot_cols, reward_cols, blocks, table, weights, rewards = refs[:7]
    value_sums, grad_sums = refs[7 : 7 + SUMS], refs[7 + SUMS : 7 + 2 * SUMS]
    sems, block_sems = refs[7 + 2 * SUMS :]
    own_row, own_col = lax.axis_index("row"), lax.axis_index("col")
    own_chip, core = own_col // 2, own_col % 2
    row_cells, col_cells = weights.shape[0] - 1, rewards.shape[0] - 1

    pairs = ((slot_rows_there, slot_rows), (slot_cols_there, slot_cols), (reward_cols_there, reward_cols))
    copies = [pltpu.make_async_copy(there, here, sems.at[at]) for at, (there, here) in enumerate(pairs)]
    for copy in copies:
        copy.start()

    def block_copy(chunk):
        part = pl.ds(pl.multiple_of(chunk * CHUNK, CHUNK), CHUNK)
        return pltpu.make_async_copy(blocks_there.at[:, :, part], blocks.at[:, :, part], block_sems.at[chunk])

    chunk_count = blocks.shape[2] // CHUNK
    for chunk in range(chunk_count):
        block_copy(chunk).start()
    for sums in (*value_sums, *grad_sums):
        sums[...] = jnp.zeros_like(sums)
    weights[row_cells] = jnp.zeros((REWARDS, BLK), jnp.bfloat16)
    rewards[col_cells] = jnp.zeros((REWARDS, BLK), jnp.bfloat16)

    owned = row_cells // n_col
    group = table.shape[0] // n_row
    pieces = REWARDS // 2 // group
    width = col_cells * BLK // pieces

    def take(shards, tables, my_half):
        for step in range(n_chip):
            for half in range(2):
                first = (2 * (own_chip ^ step) + half) * owned
                for at in range(owned):
                    lane = (half * 2 * owned + 2 * at + my_half) * BLK
                    weights[first + at] = shards[step][:, lane : lane + BLK]
        for step in range(n_row):
            for at in range(pieces):
                part = tables[step][...].astype(jnp.float32)
                line = my_half * (REWARDS // 2) + at * group
                table[step * group : (step + 1) * group, at * width : (at + 1) * width] = part[line : line + group]

    @pl.when(core == 0)
    def _():
        take(mine, others, 0)

    @pl.when(core == 1)
    def _():
        take(others, mine, 1)

    for copy in copies:
        copy.wait()
    candidates = group * n_row
    lane = lax.broadcasted_iota(jnp.int32, (REWARDS, candidates), 1)
    column = lane % group + (own_row ^ (lane // group)) * group
    line = lax.broadcasted_iota(jnp.int32, (REWARDS, candidates), 0)
    wanted = jnp.zeros((REWARDS, candidates), jnp.int32)
    for k in range(REWARDS):
        wanted = jnp.where(line == k, reward_cols[k], wanted)
    pick = (column == wanted).astype(jnp.float32).astype(jnp.bfloat16)
    for col in range(col_cells):
        rewards[col] = jnp.dot(
            pick,
            table[:, col * BLK : (col + 1) * BLK].astype(jnp.bfloat16),
            preferred_element_type=jnp.float32,
        ).astype(jnp.bfloat16)

    live_count = counts[0, 0]

    def visit(chunk, carry):
        block_copy(chunk).wait()
        found = []
        for quad in range(CHUNK // 4):
            start = chunk * CHUNK + quad * 4
            rows, cols = [], []
            for at in range(4):
                live = start + at < live_count
                rows.append(jnp.where(live, slot_rows[0, 0, start + at] // 2, row_cells))
                cols.append(jnp.where(live, slot_cols[0, 0, start + at], col_cells))
            stored = [blocks[0, 0, start + at] for at in range(4)]
            tile = jnp.concatenate(
                [jnp.concatenate(stored[:2], axis=0), jnp.concatenate(stored[2:], axis=0)], axis=1
            )
            factor = [weights[row] for row in rows]
            product = lax.dot_general(
                spread((factor[0], factor[2]), (factor[1], factor[3])),
                tile,
                (((1,), (0,)), ((), ())),
                preferred_element_type=jnp.float32,
            )
            for piece, (at, side) in enumerate(((0, 0), (2, 1), (1, 0), (3, 1))):
                part = product[piece * REWARDS : (piece + 1) * REWARDS, side * BLK : (side + 1) * BLK]
                found.append((grad_sums[at % SUMS], cols[at], part))
            factor = [rewards[col] for col in cols]
            product = lax.dot_general(
                spread((factor[0], factor[1]), (factor[2], factor[3])),
                tile,
                (((1,), (1,)), ((), ())),
                preferred_element_type=jnp.float32,
            )
            for piece, (at, side) in enumerate(((0, 0), (1, 1), (2, 0), (3, 1))):
                part = product[piece * REWARDS : (piece + 1) * REWARDS, side * BLK : (side + 1) * BLK]
                found.append((value_sums[at % SUMS], rows[at], part))
        for sums, cell, part in found:
            sums[cell] += part
        return carry

    live_chunks = (live_count + CHUNK - 1) // CHUNK
    lax.fori_loop(0, live_chunks, visit, 0)
    lax.fori_loop(live_chunks, chunk_count, lambda chunk, carry: (block_copy(chunk).wait(), carry)[1], 0)

    lines = REWARDS // n_row
    part = row_cells // n_chip

    def put_grad(step, out):
        for col in range(col_cells):
            here = pl.ds((own_row ^ step) * lines, lines)
            at, line = divmod(col * lines, REWARDS)
            out[at, line : line + lines, :] = sum(sums[col, here, :] for sums in grad_sums)

    def put_value(step, out):
        cells = pl.ds((own_chip ^ step) * part, part)
        out[:part] = sum(sums[cells] for sums in value_sums)

    def put(values, grads):
        for step in range(steps):
            if step < n_chip:
                put_value(step, values[step])
            if step < n_row:
                put_grad(step, grads[step])

    @pl.when(core == 0)
    def _():
        put(keeps, gives)

    @pl.when(core == 1)
    def _():
        put(gives, keeps)


def pair_kernel(*refs):
    count = len(refs) // 3
    for keep, got, out in zip(refs[:count], refs[count : 2 * count], refs[2 * count :]):
        half = keep.shape[0]
        out[:half], out[half:] = by_core(keep[...], got[...])


def total_kernel(n_row, n_chip, *refs):
    parts, (keep, give) = refs[:-2], refs[-2:]
    core = lax.axis_index("col") % 2
    half = keep.shape[0]

    @pl.when(core == 0)
    def _():
        total = sum(part[...] for part in parts[:n_chip])
        cut = half // 2
        keep[:cut], keep[cut:] = total[:cut], total[half : half + cut]
        give[:cut], give[cut:] = total[cut:half], total[half + cut :]

    @pl.when(core == 1)
    def _():
        total = sum(part[...] for part in parts[:n_row])
        give[...], keep[...] = total[:half], total[half:]


def result_kernel(keep, got, value, grad):
    core = lax.axis_index("col") % 2
    lines = grad.shape[0]

    def write(values, grads):
        owned = value.shape[1] // BLK // 2
        for at in range(owned):
            for parity in range(2):
                cell = 2 * at + parity
                value[:, cell * BLK : (cell + 1) * BLK] = values[parity * owned + at]
        for col in range(grad.shape[1] // BLK):
            at, line = divmod(col * lines, REWARDS)
            grad[:, col * BLK : (col + 1) * BLK] = grads[at, line : line + lines, :]

    @pl.when(core == 0)
    def _():
        write(keep, got)

    @pl.when(core == 1)
    def _():
        write(got, keep)


def on_device(n_row, n_col, blocks, slot_rows, slot_cols, counts, reward_table, reward_cols, cotangent):
    n_chip = n_col // 2
    row_cells = n_col * (cotangent.shape[1] // BLK) // 2
    col_cells = reward_table.shape[1] // BLK
    smem = pl.BlockSpec(memory_space=pltpu.SMEM)
    hbm = pl.BlockSpec(memory_space=pltpu.HBM)
    vmem = pl.BlockSpec(memory_space=pltpu.VMEM)
    in_hbm = functools.partial(pltpu.with_memory_space_constraint, memory_space=pltpu.HBM)

    steps = max(n_row, n_chip)
    small = pltpu.CompilerParams(vmem_limit_bytes=8 * 2**20)

    def swap(part):
        return lax.ppermute(part, "col", peers(n_col, 1))

    def cross(part, step):
        return lax.ppermute(part, ("row", "col"), crossings(n_row, n_col, step))

    width = 2 * reward_table.shape[0] * reward_table.shape[1] // REWARDS
    chip_inputs = pl.pallas_call(
        gather_kernel,
        out_shape=jax.ShapeDtypeStruct((REWARDS, width), cotangent.dtype),
        in_specs=[hbm] * 2 + [vmem] * 2,
        out_specs=vmem,
        scratch_shapes=[
            pltpu.VMEM(cotangent.shape, cotangent.dtype),
            pltpu.VMEM(reward_table.shape, reward_table.dtype),
            pltpu.SemaphoreType.DMA((2,)),
        ],
        compiler_params=small,
    )(in_hbm(cotangent), in_hbm(reward_table), swap(cotangent), swap(reward_table))
    mine = [chip_inputs] + [cross(chip_inputs, step) for step in range(1, steps)]
    others = [swap(part) for part in mine]

    lines, part = REWARDS // n_row, row_cells // n_chip
    tiles = jax.ShapeDtypeStruct((max(part, col_cells * lines // REWARDS), REWARDS, BLK), jnp.float32)
    both = jax.ShapeDtypeStruct((2 * tiles.shape[0], REWARDS, BLK), jnp.float32)
    sums = pl.pallas_call(
        functools.partial(products_kernel, n_row, n_col),
        out_shape=[tiles] * (2 * steps),
        in_specs=[smem] + [hbm] * 4 + [vmem] * (2 * steps),
        out_specs=[vmem] * (2 * steps),
        scratch_shapes=[
            pltpu.SMEM(slot_rows.shape, jnp.int32),
            pltpu.SMEM(slot_cols.shape, jnp.int32),
            pltpu.SMEM(reward_cols.shape, jnp.int32),
            pltpu.VMEM(blocks.shape, blocks.dtype),
            pltpu.VMEM((reward_table.shape[0] * n_row, col_cells * BLK), jnp.float32),
            pltpu.VMEM((row_cells + 1, REWARDS, BLK), jnp.bfloat16),
            pltpu.VMEM((col_cells + 1, REWARDS, BLK), jnp.bfloat16),
            *[pltpu.VMEM((row_cells + 1, REWARDS, BLK), jnp.float32)] * SUMS,
            *[pltpu.VMEM((col_cells + 1, REWARDS, BLK), jnp.float32)] * SUMS,
            pltpu.SemaphoreType.DMA((3,)),
            pltpu.SemaphoreType.DMA((blocks.shape[2] // CHUNK,)),
        ],
        compiler_params=pltpu.CompilerParams(vmem_limit_bytes=VMEM_LIMIT),
        cost_estimate=pl.CostEstimate(
            flops=4 * REWARDS * blocks.size, bytes_accessed=4 * blocks.size, transcendentals=0
        ),
    )(counts, *map(in_hbm, (slot_rows, slot_cols, reward_cols, blocks)), *mine, *others)
    keeps, gives = sums[:steps], sums[steps:]
    pairs = pl.pallas_call(
        pair_kernel,
        out_shape=[both] * steps,
        in_specs=[vmem] * (2 * steps),
        out_specs=[vmem] * steps,
        compiler_params=small,
    )(*keeps, *[swap(give) for give in gives])
    parts = [pairs[0]] + [cross(pairs[step], step) for step in range(1, steps)]
    keep, give = pl.pallas_call(
        functools.partial(total_kernel, n_row, n_chip),
        out_shape=[tiles] * 2,
        in_specs=[vmem] * steps,
        out_specs=[vmem] * 2,
        compiler_params=small,
    )(*parts)
    return pl.pallas_call(
        result_kernel,
        out_shape=[
            jax.ShapeDtypeStruct((REWARDS, part * BLK), jnp.float32),
            jax.ShapeDtypeStruct((lines, col_cells * BLK), jnp.float32),
        ],
        in_specs=[vmem] * 2,
        out_specs=[vmem] * 2,
        compiler_params=small,
    )(keep, swap(give))


def solution(mesh):
    placed = (
        P("row", "col", None, None, None),
        P("row", "col", None),
        P("row", "col", None),
        P("row", "col"),
        P("row", "col"),
        P(),
        P(None, ("row", "col")),
    )
    return jax.shard_map(
        functools.partial(on_device, mesh.shape["row"], mesh.shape["col"]),
        mesh=mesh,
        in_specs=placed,
        out_specs=(P(None, ("row", "col")), P("row", "col")),
        check_vma=False,
    )
```

```python
import functools

import jax
import jax.numpy as jnp
from jax import lax
from jax.experimental import pallas as pl
from jax.experimental.pallas import tpu as pltpu
from jax.sharding import PartitionSpec as P

BLK = 128
REWARDS = 16
CHUNK = 128
PART = 32
SUMS = 1
LAG = 2
DEEP = 4
VMEM_LIMIT = 40 * 2**20


def peers(size, step):
    return [(here, here ^ step) for here in range(size)]


def crossings(n_row, n_col, step):
    pairs = []
    for row in range(n_row):
        for chip in range(n_col // 2):
            if step < n_col // 2:
                pairs.append((row * n_col + 2 * chip, row * n_col + 2 * (chip ^ step)))
            if step < n_row:
                pairs.append((row * n_col + 2 * chip + 1, (row ^ step) * n_col + 2 * chip + 1))
    return pairs


def by_core(here, there):
    first = lax.axis_index("col") % 2 == 0
    return jnp.where(first, here, there), jnp.where(first, there, here)


def lay(table, width):
    pieces = table.shape[1] // width
    return jnp.concatenate([table[:, at * width : (at + 1) * width] for at in range(pieces)], axis=0)


def load_kernel(shard_there, table_there, shard, table, sems):
    copies = [
        pltpu.make_async_copy(shard_there, shard, sems.at[0]),
        pltpu.make_async_copy(table_there, table, sems.at[1]),
    ]
    for copy in copies:
        copy.start()
    for copy in copies:
        copy.wait()


def gather_kernel(shard, table, other_shard, other_table, mine, other):
    core, span, width = lax.axis_index("col") % 2, shard.shape[1], mine.shape[1]

    def write(shards, tables, shards_out, tables_out):
        for half in range(2):
            shards_out[:, half * span : (half + 1) * span] = shards[half][...]
        lines = [lay(part[...].astype(jnp.float32), width) for part in tables]
        tables_out[...] = jnp.concatenate(lines, axis=0).astype(tables_out.dtype)

    @pl.when(core == 0)
    def _():
        write((shard, other_shard), (table, other_table), mine, other)

    @pl.when(core == 1)
    def _():
        write((other_shard, shard), (other_table, table), other, mine)


def spread(first, second):
    empty = jnp.zeros((2 * REWARDS, BLK), jnp.bfloat16)
    top = jnp.concatenate([jnp.concatenate(first, axis=0), empty], axis=1)
    bottom = jnp.concatenate([empty, jnp.concatenate(second, axis=0)], axis=1)
    return jnp.concatenate([top, bottom], axis=0)


def products_kernel(n_row, n_col, *refs):
    n_chip = n_col // 2
    steps = max(n_row, n_chip)
    counts, slot_rows_there, slot_cols_there, reward_cols_there, blocks_there = refs[:5]
    mine, others = refs[5 : 5 + steps], refs[5 + steps : 5 + 2 * steps]
    keeps, gives = refs[5 + 2 * steps : 5 + 3 * steps], refs[5 + 3 * steps : 5 + 4 * steps]
    refs = refs[5 + 4 * steps :]
    slot_rows, slot_cols, reward_cols, blocks, table, weights, rewards = refs[:7]
    value_sums, grad_sums = refs[7 : 7 + SUMS], refs[7 + SUMS : 7 + 2 * SUMS]
    sems, block_sems = refs[7 + 2 * SUMS :]
    own_row, own_col = lax.axis_index("row"), lax.axis_index("col")
    own_chip, core = own_col // 2, own_col % 2
    row_cells, col_cells = weights.shape[0] - 1, rewards.shape[0] - 1

    pairs = ((slot_rows_there, slot_rows), (slot_cols_there, slot_cols), (reward_cols_there, reward_cols))
    copies = [pltpu.make_async_copy(there, here, sems.at[at]) for at, (there, here) in enumerate(pairs)]
    for copy in copies:
        copy.start()

    def block_copy(part):
        slots = pl.ds(pl.multiple_of(part * PART, PART), PART)
        return pltpu.make_async_copy(blocks_there.at[:, :, slots], blocks.at[:, :, slots], block_sems.at[part])

    part_count = blocks.shape[2] // PART
    for part in range(part_count):
        block_copy(part).start()
    for sums in (*value_sums, *grad_sums):
        sums[...] = jnp.zeros_like(sums)
    weights[row_cells] = jnp.zeros((REWARDS, BLK), jnp.bfloat16)
    rewards[col_cells] = jnp.zeros((REWARDS, BLK), jnp.bfloat16)

    owned = row_cells // n_col
    group = table.shape[0] // n_row
    pieces = REWARDS // 2 // group
    width = col_cells * BLK // pieces

    def take(shards, tables, my_half):
        for step in range(n_chip):
            for half in range(2):
                first = (2 * (own_chip ^ step) + half) * owned
                for at in range(owned):
                    lane = (half * 2 * owned + 2 * at + my_half) * BLK
                    weights[first + at] = shards[step][:, lane : lane + BLK]
        for step in range(n_row):
            for at in range(pieces):
                part = tables[step][...].astype(jnp.float32)
                line = my_half * (REWARDS // 2) + at * group
                table[step * group : (step + 1) * group, at * width : (at + 1) * width] = part[line : line + group]

    @pl.when(core == 0)
    def _():
        take(mine, others, 0)

    @pl.when(core == 1)
    def _():
        take(others, mine, 1)

    for copy in copies:
        copy.wait()
    candidates, side = group * n_row, 2 * BLK
    bands = side // candidates
    lane = lax.broadcasted_iota(jnp.int32, (REWARDS, side), 1)
    at = lane % candidates
    column = at % group + (own_row ^ (at // group)) * group
    line = lax.broadcasted_iota(jnp.int32, (REWARDS, side), 0)
    wanted = jnp.zeros((REWARDS, side), jnp.int32)
    for k in range(REWARDS):
        wanted = jnp.where(line == k, reward_cols[k], wanted)
    hit = column == wanted
    pick = [jnp.where(hit & (lane // candidates == band), 1.0, 0.0) for band in range(bands)]
    pick = jnp.concatenate(pick, axis=0).astype(jnp.bfloat16)

    def pick_rewards(*units):
        for turn in range(col_cells * BLK // (bands * side)):
            unit = turn % 2
            lanes = [pl.ds((turn * bands + band) * side, side) for band in range(bands)]
            tile = jnp.concatenate([table[:, here] for here in lanes], axis=0).astype(jnp.bfloat16)
            pltpu.matmul_push_rhs(tile, 0, unit)
            pltpu.matmul_acc_lhs(units[unit], pick, load_staged_rhs=0)
            product = pltpu.matmul_pop(units[unit]).astype(jnp.bfloat16)
            for cell in range(2 * bands):
                band, half = divmod(cell, 2)
                rewards[turn * 2 * bands + cell] = product[
                    band * REWARDS : (band + 1) * REWARDS, half * BLK : (half + 1) * BLK
                ]

    pl.run_scoped(pick_rewards, *[pltpu.ACC(unit)((bands * REWARDS, side), jnp.float32) for unit in (0, 1)])

    live_count = counts[0, 0]

    def visit(units, chunk, carry):
        queued = []

        def add_next():
            totals, order, cells, unit = queued.pop(0)
            product = pltpu.matmul_pop(unit)
            for piece, (at, side) in enumerate(order):
                part = product[piece * REWARDS : (piece + 1) * REWARDS, side * BLK : (side + 1) * BLK]
                totals[at % SUMS][cells[at]] += part

        for quad in range(CHUNK // 4):
            start = chunk * CHUNK + quad * 4
            if quad * 4 % PART == 0:
                block_copy(chunk * (CHUNK // PART) + quad * 4 // PART).wait()
            rows, cols = [], []
            for at in range(4):
                live = start + at < live_count
                rows.append(jnp.where(live, slot_rows[0, 0, start + at] // 2, row_cells))
                cols.append(jnp.where(live, slot_cols[0, 0, start + at], col_cells))
            stored = [blocks[0, 0, start + at] for at in range(4)]
            tile = jnp.concatenate(
                [jnp.concatenate(stored[:2], axis=0), jnp.concatenate(stored[2:], axis=0)], axis=1
            )
            plain, turned, stage = quad % 2, 1 - quad % 2, quad % 2
            pltpu.matmul_push_rhs(tile, stage, plain)
            pltpu.matmul_push_rhs(tile, stage, turned, transpose=True)
            factor = [weights[row] for row in rows]
            unit = units[plain][quad % DEEP]
            left = spread((factor[0], factor[2]), (factor[1], factor[3]))
            pltpu.matmul_acc_lhs(unit, left, load_staged_rhs=stage)
            queued.append((grad_sums, ((0, 0), (2, 1), (1, 0), (3, 1)), cols, unit))
            factor = [rewards[col] for col in cols]
            unit = units[turned][quad % DEEP]
            left = spread((factor[0], factor[1]), (factor[2], factor[3]))
            pltpu.matmul_acc_lhs(unit, left, load_staged_rhs=stage)
            queued.append((value_sums, ((0, 0), (1, 1), (2, 0), (3, 1)), rows, unit))
            while len(queued) > 2 * LAG:
                add_next()
        while queued:
            add_next()
        return carry

    live_chunks = (live_count + CHUNK - 1) // CHUNK

    def multiply(*units):
        held = (units[:DEEP], units[DEEP:])
        lax.fori_loop(0, live_chunks, functools.partial(visit, held), 0)

    pl.run_scoped(multiply, *[pltpu.ACC(unit)((4 * REWARDS, 2 * BLK), jnp.float32) for unit in (0, 1) for _ in range(DEEP)])
    lax.fori_loop(
        live_chunks * (CHUNK // PART), part_count, lambda part, carry: (block_copy(part).wait(), carry)[1], 0
    )

    lines = REWARDS // n_row
    part = row_cells // n_chip

    def put_grad(step, out):
        for col in range(col_cells):
            here = pl.ds((own_row ^ step) * lines, lines)
            at, line = divmod(col * lines, REWARDS)
            out[at, line : line + lines, :] = sum(sums[col, here, :] for sums in grad_sums)

    def put_value(step, out):
        cells = pl.ds((own_chip ^ step) * part, part)
        out[:part] = sum(sums[cells] for sums in value_sums)

    def put(values, grads):
        for step in range(steps):
            if step < n_chip:
                put_value(step, values[step])
            if step < n_row:
                put_grad(step, grads[step])

    @pl.when(core == 0)
    def _():
        put(keeps, gives)

    @pl.when(core == 1)
    def _():
        put(gives, keeps)


def pair_kernel(keep, got, out):
    half = keep.shape[0]
    out[:half], out[half:] = by_core(keep[...], got[...])


def total_kernel(n_row, n_chip, *refs):
    parts, (keep, give) = refs[:-2], refs[-2:]
    core = lax.axis_index("col") % 2
    half = keep.shape[0]

    @pl.when(core == 0)
    def _():
        total = sum(part[...] for part in parts[:n_chip])
        cut = half // 2
        keep[:cut], keep[cut:] = total[:cut], total[half : half + cut]
        give[:cut], give[cut:] = total[cut:half], total[half + cut :]

    @pl.when(core == 1)
    def _():
        total = sum(part[...] for part in parts[:n_row])
        give[...], keep[...] = total[:half], total[half:]


def result_kernel(keep, got, value, grad):
    core = lax.axis_index("col") % 2
    lines = grad.shape[0]

    def write(values, grads):
        owned = value.shape[1] // BLK // 2
        for at in range(owned):
            for parity in range(2):
                cell = 2 * at + parity
                value[:, cell * BLK : (cell + 1) * BLK] = values[parity * owned + at]
        for col in range(grad.shape[1] // BLK):
            at, line = divmod(col * lines, REWARDS)
            grad[:, col * BLK : (col + 1) * BLK] = grads[at, line : line + lines, :]

    @pl.when(core == 0)
    def _():
        write(keep, got)

    @pl.when(core == 1)
    def _():
        write(got, keep)


def on_device(n_row, n_col, blocks, slot_rows, slot_cols, counts, reward_table, reward_cols, cotangent):
    n_chip = n_col // 2
    row_cells = n_col * (cotangent.shape[1] // BLK) // 2
    col_cells = reward_table.shape[1] // BLK
    smem = pl.BlockSpec(memory_space=pltpu.SMEM)
    hbm = pl.BlockSpec(memory_space=pltpu.HBM)
    vmem = pl.BlockSpec(memory_space=pltpu.VMEM)
    in_hbm = functools.partial(pltpu.with_memory_space_constraint, memory_space=pltpu.HBM)

    steps = max(n_row, n_chip)
    small = pltpu.CompilerParams(vmem_limit_bytes=8 * 2**20)

    def swap(part):
        return lax.ppermute(part, "col", peers(n_col, 1))

    def cross(part, step):
        return lax.ppermute(part, ("row", "col"), crossings(n_row, n_col, step))

    width = 2 * reward_table.shape[0] * reward_table.shape[1] // REWARDS
    loaded = pl.pallas_call(
        load_kernel,
        out_shape=[jax.ShapeDtypeStruct(arg.shape, arg.dtype) for arg in (cotangent, reward_table)],
        in_specs=[hbm] * 2,
        out_specs=[vmem] * 2,
        scratch_shapes=[pltpu.SemaphoreType.DMA((2,))],
        compiler_params=small,
        cost_estimate=pl.CostEstimate(flops=0, bytes_accessed=4 * 2**20, transcendentals=0),
    )(in_hbm(cotangent), in_hbm(reward_table))
    mine, other = pl.pallas_call(
        gather_kernel,
        out_shape=[jax.ShapeDtypeStruct((REWARDS, width), cotangent.dtype)] * 2,
        in_specs=[vmem] * 4,
        out_specs=[vmem] * 2,
        compiler_params=small,
    )(*loaded, swap(cotangent), swap(reward_table))
    mine = [mine] + [cross(mine, step) for step in range(1, steps)]
    others = [other] + [swap(part) for part in mine[1:]]

    lines, part = REWARDS // n_row, row_cells // n_chip
    tiles = jax.ShapeDtypeStruct((max(part, col_cells * lines // REWARDS), REWARDS, BLK), jnp.float32)
    both = jax.ShapeDtypeStruct((2 * tiles.shape[0], REWARDS, BLK), jnp.float32)
    sums = pl.pallas_call(
        functools.partial(products_kernel, n_row, n_col),
        out_shape=[tiles] * (2 * steps),
        in_specs=[smem] + [hbm] * 4 + [vmem] * (2 * steps),
        out_specs=[vmem] * (2 * steps),
        scratch_shapes=[
            pltpu.SMEM(slot_rows.shape, jnp.int32),
            pltpu.SMEM(slot_cols.shape, jnp.int32),
            pltpu.SMEM(reward_cols.shape, jnp.int32),
            pltpu.VMEM(blocks.shape, blocks.dtype),
            pltpu.VMEM((reward_table.shape[0] * n_row, col_cells * BLK), jnp.float32),
            pltpu.VMEM((row_cells + 1, REWARDS, BLK), jnp.bfloat16),
            pltpu.VMEM((col_cells + 1, REWARDS, BLK), jnp.bfloat16),
            *[pltpu.VMEM((row_cells + 1, REWARDS, BLK), jnp.float32)] * SUMS,
            *[pltpu.VMEM((col_cells + 1, REWARDS, BLK), jnp.float32)] * SUMS,
            pltpu.SemaphoreType.DMA((3,)),
            pltpu.SemaphoreType.DMA((blocks.shape[2] // PART,)),
        ],
        compiler_params=pltpu.CompilerParams(vmem_limit_bytes=VMEM_LIMIT),
        cost_estimate=pl.CostEstimate(
            flops=4 * REWARDS * blocks.size, bytes_accessed=4 * blocks.size, transcendentals=0
        ),
    )(counts, *map(in_hbm, (slot_rows, slot_cols, reward_cols, blocks)), *mine, *others)
    keeps, gives = sums[:steps], sums[steps:]
    parts = []
    for step in reversed(range(steps)):
        pair = pl.pallas_call(
            pair_kernel,
            out_shape=both,
            in_specs=[vmem] * 2,
            out_specs=vmem,
            compiler_params=small,
        )(keeps[step], swap(gives[step]))
        parts.insert(0, cross(pair, step) if step else pair)
    keep, give = pl.pallas_call(
        functools.partial(total_kernel, n_row, n_chip),
        out_shape=[tiles] * 2,
        in_specs=[vmem] * steps,
        out_specs=[vmem] * 2,
        compiler_params=small,
    )(*parts)
    return pl.pallas_call(
        result_kernel,
        out_shape=[
            jax.ShapeDtypeStruct((REWARDS, part * BLK), jnp.float32),
            jax.ShapeDtypeStruct((lines, col_cells * BLK), jnp.float32),
        ],
        in_specs=[vmem] * 2,
        out_specs=[vmem] * 2,
        compiler_params=small,
    )(keep, swap(give))


def solution(mesh):
    placed = (
        P("row", "col", None, None, None),
        P("row", "col", None),
        P("row", "col", None),
        P("row", "col"),
        P("row", "col"),
        P(),
        P(None, ("row", "col")),
    )
    return jax.shard_map(
        functools.partial(on_device, mesh.shape["row"], mesh.shape["col"]),
        mesh=mesh,
        in_specs=placed,
        out_specs=(P(None, ("row", "col")), P("row", "col")),
        check_vma=False,
    )
```

```python
import functools

import jax
import jax.numpy as jnp
from jax import lax
from jax.experimental import pallas as pl
from jax.experimental.pallas import tpu as pltpu
from jax.sharding import PartitionSpec as P

BLK = 128
REWARDS = 16
CHUNK = 128
SUMS = 1
GRAIN = 128
MOST = 32767.0
LAG = 2
DEEP = 4


def peers(size, step):
    return [(here, here ^ step) for here in range(size)]


def crossings(n_row, n_col, step):
    pairs = []
    for row in range(n_row):
        for chip in range(n_col // 2):
            if step < n_col // 2:
                pairs.append((row * n_col + 2 * chip, row * n_col + 2 * (chip ^ step)))
            if step < n_row:
                pairs.append((row * n_col + 2 * chip + 1, (row ^ step) * n_col + 2 * chip + 1))
    return pairs


def by_core(here, there):
    first = lax.axis_index("col") % 2 == 0
    return jnp.where(first, here, there), jnp.where(first, there, here)


def lay(table, width):
    pieces = table.shape[1] // width
    return jnp.concatenate([table[:, at * width : (at + 1) * width] for at in range(pieces)], axis=0)


def load_kernel(shard_there, table_there, shard, table, sems):
    copies = [
        pltpu.make_async_copy(shard_there, shard, sems.at[0]),
        pltpu.make_async_copy(table_there, table, sems.at[1]),
    ]
    for copy in copies:
        copy.start()
    for copy in copies:
        copy.wait()


def prefetch_kernel(after, rows_there, cols_there, reward_cols_there, blocks_there, rows, cols, pick, blocks, reward_cols, sems):
    pairs = (
        (reward_cols_there, reward_cols),
        (rows_there, rows),
        (cols_there, cols),
        (blocks_there, blocks),
    )
    copies = [pltpu.make_async_copy(there, here, sems.at[at]) for at, (there, here) in enumerate(pairs)]
    for copy in copies:
        copy.start()
    copies[0].wait()
    own_row = lax.axis_index("row")
    candidates = pick.shape[1] * REWARDS // pick.shape[0]
    group = candidates // lax.axis_size("row")
    lane = lax.broadcasted_iota(jnp.int32, (REWARDS, pick.shape[1]), 1)
    at = lane % candidates
    column = at % group + (own_row ^ (at // group)) * group
    line = lax.broadcasted_iota(jnp.int32, (REWARDS, pick.shape[1]), 0)
    wanted = jnp.zeros(lane.shape, jnp.int32)
    for k in range(REWARDS):
        wanted = jnp.where(line == k, reward_cols[k], wanted)
    hit = column == wanted
    bands = [jnp.where(hit & (lane // candidates == band), 1.0, 0.0) for band in range(pick.shape[1] // candidates)]
    pick[...] = jnp.concatenate(bands, axis=0).astype(jnp.bfloat16)
    for copy in copies[1:]:
        copy.wait()


def after_kernel(part, after, out):
    out[...] = part[...]


def gather_kernel(shard, table, other_shard, other_table, mine, other):
    core, span, width = lax.axis_index("col") % 2, shard.shape[1], mine.shape[1]

    def write(shards, tables, shards_out, tables_out):
        for half in range(2):
            shards_out[:, half * span : (half + 1) * span] = shards[half][...]
        lines = [lay(part[...].astype(jnp.float32), width) for part in tables]
        tables_out[...] = jnp.concatenate(lines, axis=0).astype(tables_out.dtype)

    @pl.when(core == 0)
    def _():
        write((shard, other_shard), (table, other_table), mine, other)

    @pl.when(core == 1)
    def _():
        write((other_shard, shard), (other_table, table), other, mine)


def spread(first, second):
    empty = jnp.zeros((2 * REWARDS, BLK), jnp.bfloat16)
    top = jnp.concatenate([jnp.concatenate(first, axis=0), empty], axis=1)
    bottom = jnp.concatenate([empty, jnp.concatenate(second, axis=0)], axis=1)
    return jnp.concatenate([top, bottom], axis=0)


def products_kernel(n_row, n_col, *refs):
    n_chip = n_col // 2
    steps = max(n_row, n_chip)
    counts, slot_rows_there, slot_cols_there, pick, blocks = refs[:5]
    mine, others = refs[5 : 5 + steps], refs[5 + steps : 5 + 2 * steps]
    keeps, gives = refs[5 + 2 * steps : 5 + 3 * steps], refs[5 + 3 * steps : 5 + 4 * steps]
    refs = refs[5 + 4 * steps :]
    slot_rows, slot_cols, table, weights, rewards = refs[:5]
    value_sums, grad_sums = refs[5 : 5 + SUMS], refs[5 + SUMS : 5 + 2 * SUMS]
    draft, sems = refs[5 + 2 * SUMS :]
    own_row, own_col = lax.axis_index("row"), lax.axis_index("col")
    own_chip, core = own_col // 2, own_col % 2
    row_cells, col_cells = weights.shape[0] - 1, rewards.shape[0] - 1

    pairs = ((slot_rows_there, slot_rows), (slot_cols_there, slot_cols))
    copies = [pltpu.make_async_copy(there, here, sems.at[at]) for at, (there, here) in enumerate(pairs)]
    for copy in copies:
        copy.start()

    for sums in (*value_sums, *grad_sums):
        sums[...] = jnp.zeros_like(sums)
    weights[row_cells] = jnp.zeros((REWARDS, BLK), jnp.bfloat16)
    rewards[col_cells] = jnp.zeros((REWARDS, BLK), jnp.bfloat16)

    owned = row_cells // n_col
    group = table.shape[0] // n_row
    pieces = REWARDS // 2 // group
    width = col_cells * BLK // pieces

    def take(shards, tables, my_half):
        for step in range(n_chip):
            for half in range(2):
                first = (2 * (own_chip ^ step) + half) * owned
                for at in range(owned):
                    lane = (half * 2 * owned + 2 * at + my_half) * BLK
                    weights[first + at] = shards[step][:, lane : lane + BLK]
        for step in range(n_row):
            for at in range(pieces):
                part = tables[step][...].astype(jnp.float32)
                line = my_half * (REWARDS // 2) + at * group
                table[step * group : (step + 1) * group, at * width : (at + 1) * width] = part[line : line + group]

    @pl.when(core == 0)
    def _():
        take(mine, others, 0)

    @pl.when(core == 1)
    def _():
        take(others, mine, 1)

    side = 2 * BLK
    bands = side // (group * n_row)

    def pick_rewards(*units):
        for turn in range(col_cells * BLK // (bands * side)):
            unit = turn % 2
            lanes = [pl.ds((turn * bands + band) * side, side) for band in range(bands)]
            tile = jnp.concatenate([table[:, here] for here in lanes], axis=0).astype(jnp.bfloat16)
            pltpu.matmul_push_rhs(tile, 0, unit)
            pltpu.matmul_acc_lhs(units[unit], pick[...], load_staged_rhs=0)
            product = pltpu.matmul_pop(units[unit]).astype(jnp.bfloat16)
            for cell in range(2 * bands):
                band, half = divmod(cell, 2)
                rewards[turn * 2 * bands + cell] = product[
                    band * REWARDS : (band + 1) * REWARDS, half * BLK : (half + 1) * BLK
                ]

    pl.run_scoped(pick_rewards, *[pltpu.ACC(unit)((bands * REWARDS, side), jnp.float32) for unit in (0, 1)])

    for copy in copies:
        copy.wait()
    live_count = counts[0, 0]

    def visit(units, chunk, carry):
        queued = []

        def add_next():
            totals, order, cells, unit = queued.pop(0)
            product = pltpu.matmul_pop(unit)
            for piece, (at, side) in enumerate(order):
                part = product[piece * REWARDS : (piece + 1) * REWARDS, side * BLK : (side + 1) * BLK]
                totals[at % SUMS][cells[at]] += part

        for quad in range(CHUNK // 4):
            start = chunk * CHUNK + quad * 4
            rows, cols = [], []
            for at in range(4):
                live = start + at < live_count
                rows.append(jnp.where(live, slot_rows[0, 0, start + at] // 2, row_cells))
                cols.append(jnp.where(live, slot_cols[0, 0, start + at], col_cells))
            stored = [blocks[0, 0, start + at] for at in range(4)]
            tile = jnp.concatenate(
                [jnp.concatenate(stored[:2], axis=0), jnp.concatenate(stored[2:], axis=0)], axis=1
            )
            plain, turned, stage = quad % 2, 1 - quad % 2, quad % 2
            pltpu.matmul_push_rhs(tile, stage, plain)
            pltpu.matmul_push_rhs(tile, stage, turned, transpose=True)
            factor = [weights[row] for row in rows]
            unit = units[plain][quad % DEEP]
            left = spread((factor[0], factor[2]), (factor[1], factor[3]))
            pltpu.matmul_acc_lhs(unit, left, load_staged_rhs=stage)
            queued.append((grad_sums, ((0, 0), (2, 1), (1, 0), (3, 1)), cols, unit))
            factor = [rewards[col] for col in cols]
            unit = units[turned][quad % DEEP]
            left = spread((factor[0], factor[1]), (factor[2], factor[3]))
            pltpu.matmul_acc_lhs(unit, left, load_staged_rhs=stage)
            queued.append((value_sums, ((0, 0), (1, 1), (2, 0), (3, 1)), rows, unit))
            while len(queued) > 2 * LAG:
                add_next()
        while queued:
            add_next()
        return carry

    live_chunks = (live_count + CHUNK - 1) // CHUNK

    def multiply(*units):
        held = (units[:DEEP], units[DEEP:])
        lax.fori_loop(0, live_chunks, functools.partial(visit, held), 0)

    pl.run_scoped(multiply, *[pltpu.ACC(unit)((4 * REWARDS, 2 * BLK), jnp.float32) for unit in (0, 1) for _ in range(DEEP)])

    lines = REWARDS // n_row
    part = row_cells // n_chip

    def put_grad(step, out):
        tiles = out if step == 0 else draft
        for col in range(col_cells):
            here = pl.ds((own_row ^ step) * lines, lines)
            at, line = divmod(col * lines, REWARDS)
            tiles[at, line : line + lines, :] = sum(sums[col, here, :] for sums in grad_sums)
        if step:
            encode(draft, out)

    def put_value(step, out):
        cells = pl.ds((own_chip ^ step) * part, part)
        value = sum(sums[cells] for sums in value_sums)
        if step:
            encode(value, out)
        else:
            out[...] = value

    def put(values, grads):
        for step in range(steps):
            if step < n_chip:
                put_value(step, values[step])
            if step < n_row:
                put_grad(step, grads[step])

    @pl.when(core == 0)
    def _():
        put(keeps, gives)

    @pl.when(core == 1)
    def _():
        put(gives, keeps)


def encode(tiles, out):
    values = [tiles[at] for at in range(out.shape[0] - 1)]
    top = functools.reduce(jnp.maximum, [jnp.abs(value) for value in values])
    power = jnp.ceil(jnp.log2(jnp.maximum(top, 2.0**-100)) * GRAIN)
    out[len(values)] = power.astype(jnp.int32).astype(jnp.int16)
    factor = MOST / jnp.exp2(power / GRAIN)
    for at, value in enumerate(values):
        whole = jnp.clip(jnp.round(value * factor), -MOST, MOST)
        out[at] = whole.astype(jnp.int32).astype(jnp.int16)


def decode(coded, first, count):
    power = coded[first + count].astype(jnp.int32).astype(jnp.float32)
    factor = jnp.exp2(power / GRAIN) / MOST
    return [coded[first + at].astype(jnp.int32).astype(jnp.float32) * factor for at in range(count)]


def pair_kernel(keep, got, out):
    half = keep.shape[0]
    out[:half], out[half:] = by_core(keep[...], got[...])


def total_kernel(n_row, n_chip, *refs):
    parts, (keep, give) = refs[:-2], refs[-2:]
    core = lax.axis_index("col") % 2
    half = keep.shape[0]

    def total(count, side):
        sums = [parts[0][side * half + at] for at in range(half)]
        for part in parts[1:count]:
            arrived = decode(part, side * (half + 1), half)
            sums = [one + other for one, other in zip(sums, arrived)]
        return sums

    @pl.when(core == 0)
    def _():
        cut = half // 2
        for side in range(2):
            sums = total(n_chip, side)
            for at in range(cut):
                keep[side * cut + at], give[side * cut + at] = sums[at], sums[cut + at]

    @pl.when(core == 1)
    def _():
        for side, out in enumerate((give, keep)):
            for at, one in enumerate(total(n_row, side)):
                out[at] = one


def result_kernel(keep, got, value, grad):
    core = lax.axis_index("col") % 2
    lines = grad.shape[0]

    def write(values, grads):
        owned = value.shape[1] // BLK // 2
        for at in range(owned):
            for parity in range(2):
                cell = 2 * at + parity
                value[:, cell * BLK : (cell + 1) * BLK] = values[parity * owned + at]
        for col in range(grad.shape[1] // BLK):
            at, line = divmod(col * lines, REWARDS)
            grad[:, col * BLK : (col + 1) * BLK] = grads[at, line : line + lines, :]

    @pl.when(core == 0)
    def _():
        write(keep, got)

    @pl.when(core == 1)
    def _():
        write(got, keep)


def on_device(n_row, n_col, blocks, slot_rows, slot_cols, counts, reward_table, reward_cols, cotangent):
    n_chip = n_col // 2
    row_cells = n_col * (cotangent.shape[1] // BLK) // 2
    col_cells = reward_table.shape[1] // BLK
    smem = pl.BlockSpec(memory_space=pltpu.SMEM)
    hbm = pl.BlockSpec(memory_space=pltpu.HBM)
    vmem = pl.BlockSpec(memory_space=pltpu.VMEM)
    in_hbm = functools.partial(pltpu.with_memory_space_constraint, memory_space=pltpu.HBM)

    steps = max(n_row, n_chip)
    small = pltpu.CompilerParams(vmem_limit_bytes=8 * 2**20)

    def swap(part):
        return lax.ppermute(part, "col", peers(n_col, 1))

    def cross(part, step):
        return lax.ppermute(part, ("row", "col"), crossings(n_row, n_col, step))

    width = 2 * reward_table.shape[0] * reward_table.shape[1] // REWARDS
    loaded = pl.pallas_call(
        load_kernel,
        out_shape=[jax.ShapeDtypeStruct(arg.shape, arg.dtype) for arg in (cotangent, reward_table)],
        in_specs=[hbm] * 2,
        out_specs=[vmem] * 2,
        scratch_shapes=[pltpu.SemaphoreType.DMA((2,))],
        compiler_params=small,
        cost_estimate=pl.CostEstimate(flops=0, bytes_accessed=4 * 2**20, transcendentals=0),
    )(in_hbm(cotangent), in_hbm(reward_table))
    mine, other = pl.pallas_call(
        gather_kernel,
        out_shape=[jax.ShapeDtypeStruct((REWARDS, width), cotangent.dtype)] * 2,
        in_specs=[vmem] * 4,
        out_specs=[vmem] * 2,
        compiler_params=small,
    )(*loaded, swap(cotangent), swap(reward_table))
    mine = [mine] + [cross(mine, step) for step in range(1, steps)]
    side = 2 * BLK
    rows, cols, pick, stored = pl.pallas_call(
        prefetch_kernel,
        out_shape=[
            jax.ShapeDtypeStruct(slot_rows.shape, slot_rows.dtype),
            jax.ShapeDtypeStruct(slot_cols.shape, slot_cols.dtype),
            jax.ShapeDtypeStruct((side // (reward_table.shape[0] * n_row) * REWARDS, side), jnp.bfloat16),
            jax.ShapeDtypeStruct(blocks.shape, blocks.dtype),
        ],
        in_specs=[vmem] + [hbm] * 4,
        out_specs=[vmem] * 4,
        scratch_shapes=[pltpu.SMEM(reward_cols.shape, jnp.int32), pltpu.SemaphoreType.DMA((4,))],
        compiler_params=pltpu.CompilerParams(vmem_limit_bytes=24 * 2**20),
        cost_estimate=pl.CostEstimate(flops=0, bytes_accessed=2 * blocks.size * 2, transcendentals=0),
    )(mine[0], *map(in_hbm, (slot_rows, slot_cols, reward_cols, blocks)))
    first = pl.pallas_call(
        after_kernel,
        out_shape=jax.ShapeDtypeStruct(mine[-1].shape, mine[-1].dtype),
        in_specs=[vmem] * 2,
        out_specs=vmem,
        compiler_params=small,
    )(mine[-1], pick)
    others = [other] + [swap(part) for part in (*mine[1:-1], first)]

    lines, part = REWARDS // n_row, row_cells // n_chip
    tiles = jax.ShapeDtypeStruct((max(part, col_cells * lines // REWARDS), REWARDS, BLK), jnp.float32)
    coded = jax.ShapeDtypeStruct((tiles.shape[0] + 1, REWARDS, BLK), jnp.int16)
    sums = pl.pallas_call(
        functools.partial(products_kernel, n_row, n_col),
        out_shape=[tiles, *[coded] * (steps - 1)] * 2,
        in_specs=[smem] + [vmem] * (4 + 2 * steps),
        out_specs=[vmem] * (2 * steps),
        scratch_shapes=[
            pltpu.SMEM(slot_rows.shape, jnp.int32),
            pltpu.SMEM(slot_cols.shape, jnp.int32),
            pltpu.VMEM((reward_table.shape[0] * n_row, col_cells * BLK), jnp.float32),
            pltpu.VMEM((row_cells + 1, REWARDS, BLK), jnp.bfloat16),
            pltpu.VMEM((col_cells + 1, REWARDS, BLK), jnp.bfloat16),
            *[pltpu.VMEM((row_cells + 1, REWARDS, BLK), jnp.float32)] * SUMS,
            *[pltpu.VMEM((col_cells + 1, REWARDS, BLK), jnp.float32)] * SUMS,
            pltpu.VMEM(tiles.shape, jnp.float32),
            pltpu.SemaphoreType.DMA((2,)),
        ],
        compiler_params=pltpu.CompilerParams(vmem_limit_bytes=24 * 2**20),
        cost_estimate=pl.CostEstimate(
            flops=4 * REWARDS * blocks.size, bytes_accessed=4 * blocks.size, transcendentals=0
        ),
    )(counts, rows, cols, pick, stored, *mine, *others)
    keeps, gives = sums[:steps], sums[steps:]
    parts = []
    for step in reversed(range(steps)):
        pair = pl.pallas_call(
            pair_kernel,
            out_shape=jax.ShapeDtypeStruct((2 * keeps[step].shape[0], REWARDS, BLK), keeps[step].dtype),
            in_specs=[vmem] * 2,
            out_specs=vmem,
            compiler_params=small,
        )(keeps[step], swap(gives[step]))
        parts.insert(0, cross(pair, step) if step else pair)
    keep, give = pl.pallas_call(
        functools.partial(total_kernel, n_row, n_chip),
        out_shape=[tiles] * 2,
        in_specs=[vmem] * steps,
        out_specs=[vmem] * 2,
        compiler_params=small,
    )(*parts)
    return pl.pallas_call(
        result_kernel,
        out_shape=[
            jax.ShapeDtypeStruct((REWARDS, part * BLK), jnp.float32),
            jax.ShapeDtypeStruct((lines, col_cells * BLK), jnp.float32),
        ],
        in_specs=[vmem] * 2,
        out_specs=[vmem] * 2,
        compiler_params=small,
    )(keep, swap(give))


def solution(mesh):
    placed = (
        P("row", "col", None, None, None),
        P("row", "col", None),
        P("row", "col", None),
        P("row", "col"),
        P("row", "col"),
        P(),
        P(None, ("row", "col")),
    )
    return jax.shard_map(
        functools.partial(on_device, mesh.shape["row"], mesh.shape["col"]),
        mesh=mesh,
        in_specs=placed,
        out_specs=(P(None, ("row", "col")), P("row", "col")),
        check_vma=False,
    )
```

```python
import functools

import jax
import jax.numpy as jnp
from jax import lax
from jax.experimental import pallas as pl
from jax.experimental.pallas import tpu as pltpu
from jax.sharding import PartitionSpec as P

BLK = 128
REWARDS = 16
LATE = 128
SUMS = 1
GRAIN = 128
MOST = 32767.0
SPARE = 8
LAG = 2
DEEP = 4


def peers(size, step):
    return [(here, here ^ step) for here in range(size)]


def crossings(n_row, n_col, step):
    pairs = []
    for row in range(n_row):
        for chip in range(n_col // 2):
            if step < n_col // 2:
                pairs.append((row * n_col + 2 * chip, row * n_col + 2 * (chip ^ step)))
            if step < n_row:
                pairs.append((row * n_col + 2 * chip + 1, (row ^ step) * n_col + 2 * chip + 1))
    return pairs


def by_core(here, there):
    first = lax.axis_index("col") % 2 == 0
    return jnp.where(first, here, there), jnp.where(first, there, here)


def lay(table, width):
    pieces = table.shape[1] // width
    return jnp.concatenate([table[:, at * width : (at + 1) * width] for at in range(pieces)], axis=0)


def load_kernel(shard_there, table_there, shard, table, sems):
    copies = [
        pltpu.make_async_copy(shard_there, shard, sems.at[0]),
        pltpu.make_async_copy(table_there, table, sems.at[1]),
    ]
    for copy in copies:
        copy.start()
    for copy in copies:
        copy.wait()


def prefetch_kernel(after, rows_there, cols_there, reward_cols_there, blocks_there, rows, cols, pick, blocks, reward_cols, sems):
    pairs = (
        (reward_cols_there, reward_cols),
        (rows_there, rows),
        (cols_there, cols),
        (blocks_there.at[:, :, pl.ds(0, blocks.shape[2])], blocks),
    )
    copies = [pltpu.make_async_copy(there, here, sems.at[at]) for at, (there, here) in enumerate(pairs)]
    for copy in copies:
        copy.start()
    copies[0].wait()
    own_row = lax.axis_index("row")
    candidates = pick.shape[1] * REWARDS // pick.shape[0]
    group = candidates // lax.axis_size("row")
    lane = lax.broadcasted_iota(jnp.int32, (REWARDS, pick.shape[1]), 1)
    at = lane % candidates
    column = at % group + (own_row ^ (at // group)) * group
    line = lax.broadcasted_iota(jnp.int32, (REWARDS, pick.shape[1]), 0)
    wanted = jnp.zeros(lane.shape, jnp.int32)
    for k in range(REWARDS):
        wanted = jnp.where(line == k, reward_cols[k], wanted)
    hit = column == wanted
    bands = [jnp.where(hit & (lane // candidates == band), 1.0, 0.0) for band in range(pick.shape[1] // candidates)]
    pick[...] = jnp.concatenate(bands, axis=0).astype(jnp.bfloat16)
    for copy in copies[1:]:
        copy.wait()


def after_kernel(part, after, out):
    out[...] = part[...]


def gather_kernel(shard, table, other_shard, other_table, mine, other):
    core, span, width = lax.axis_index("col") % 2, shard.shape[1], mine.shape[1]

    def write(shards, tables, shards_out, tables_out):
        for half in range(2):
            shards_out[:, half * span : (half + 1) * span] = shards[half][...]
        lines = [lay(part[...].astype(jnp.float32), width) for part in tables]
        tables_out[...] = jnp.concatenate(lines, axis=0).astype(tables_out.dtype)

    @pl.when(core == 0)
    def _():
        write((shard, other_shard), (table, other_table), mine, other)

    @pl.when(core == 1)
    def _():
        write((other_shard, shard), (other_table, table), other, mine)


def spread(first, second):
    empty = jnp.zeros((2 * REWARDS, BLK), jnp.bfloat16)
    top = jnp.concatenate([jnp.concatenate(first, axis=0), empty], axis=1)
    bottom = jnp.concatenate([empty, jnp.concatenate(second, axis=0)], axis=1)
    return jnp.concatenate([top, bottom], axis=0)


def products_kernel(n_row, n_col, *refs):
    n_chip = n_col // 2
    steps = max(n_row, n_chip)
    counts, slot_rows, slot_cols, blocks_there, pick, blocks = refs[:6]
    mine, others = refs[6 : 6 + steps], refs[6 + steps : 6 + 2 * steps]
    keeps, gives = refs[6 + 2 * steps : 6 + 3 * steps], refs[6 + 3 * steps : 6 + 4 * steps]
    refs = refs[6 + 4 * steps :]
    table, weights, rewards = refs[:3]
    value_sums, grad_sums = refs[3 : 3 + SUMS], refs[3 + SUMS : 3 + 2 * SUMS]
    draft, late, late_sem = refs[3 + 2 * SUMS :]
    own_row, own_col = lax.axis_index("row"), lax.axis_index("col")
    own_chip, core = own_col // 2, own_col % 2
    row_cells, col_cells = weights.shape[0] - SPARE, rewards.shape[0] - SPARE

    early = blocks.shape[2]
    late_copy = pltpu.make_async_copy(blocks_there.at[:, :, pl.ds(early, LATE)], late, late_sem)
    late_copy.start()
    for sums in (*value_sums, *grad_sums):
        sums[...] = jnp.zeros_like(sums)
    for spare in range(SPARE):
        weights[row_cells + spare] = jnp.zeros((REWARDS, BLK), jnp.bfloat16)
        rewards[col_cells + spare] = jnp.zeros((REWARDS, BLK), jnp.bfloat16)

    owned = row_cells // n_col
    group = table.shape[0] // n_row
    pieces = REWARDS // 2 // group
    width = col_cells * BLK // pieces

    def take(shards, tables, my_half):
        for step in range(n_chip):
            for half in range(2):
                first = (2 * (own_chip ^ step) + half) * owned
                for at in range(owned):
                    lane = (half * 2 * owned + 2 * at + my_half) * BLK
                    weights[first + at] = shards[step][:, lane : lane + BLK]
        for step in range(n_row):
            for at in range(pieces):
                part = tables[step][...].astype(jnp.float32)
                line = my_half * (REWARDS // 2) + at * group
                table[step * group : (step + 1) * group, at * width : (at + 1) * width] = part[line : line + group]

    @pl.when(core == 0)
    def _():
        take(mine, others, 0)

    @pl.when(core == 1)
    def _():
        take(others, mine, 1)

    side = 2 * BLK
    bands = side // (group * n_row)

    def pick_rewards(*units):
        for turn in range(col_cells * BLK // (bands * side)):
            unit = turn % 2
            lanes = [pl.ds((turn * bands + band) * side, side) for band in range(bands)]
            tile = jnp.concatenate([table[:, here] for here in lanes], axis=0).astype(jnp.bfloat16)
            pltpu.matmul_push_rhs(tile, 0, unit)
            pltpu.matmul_acc_lhs(units[unit], pick[...], load_staged_rhs=0)
            product = pltpu.matmul_pop(units[unit]).astype(jnp.bfloat16)
            for cell in range(2 * bands):
                band, half = divmod(cell, 2)
                rewards[turn * 2 * bands + cell] = product[
                    band * REWARDS : (band + 1) * REWARDS, half * BLK : (half + 1) * BLK
                ]

    pl.run_scoped(pick_rewards, *[pltpu.ACC(unit)((bands * REWARDS, side), jnp.float32) for unit in (0, 1)])

    live_count = counts[0, 0]

    def multiply(*held):
        units = (held[:DEEP], held[DEEP:])
        queued = []

        def add_next():
            totals, order, cells, unit = queued.pop(0)
            product = pltpu.matmul_pop(unit)
            for piece, (at, side) in enumerate(order):
                part = product[piece * REWARDS : (piece + 1) * REWARDS, side * BLK : (side + 1) * BLK]
                totals[at % SUMS][cells[at]] += part

        for quad in range((early + LATE) // 4):
            start = quad * 4
            if start == early:
                late_copy.wait()
            rows, cols = [], []
            for at in range(4):
                live = start + at < live_count
                rows.append(jnp.where(live, slot_rows[0, 0, start + at] // 2, row_cells + (start + at) % SPARE))
                cols.append(jnp.where(live, slot_cols[0, 0, start + at], col_cells + (start + at) % SPARE))
            held_in, first = (blocks, start) if start < early else (late, start - early)
            stored = [held_in[0, 0, first + at] for at in range(4)]
            tile = jnp.concatenate(
                [jnp.concatenate(stored[:2], axis=0), jnp.concatenate(stored[2:], axis=0)], axis=1
            )
            plain, turned, stage = quad % 2, 1 - quad % 2, quad % 2
            pltpu.matmul_push_rhs(tile, stage, plain)
            pltpu.matmul_push_rhs(tile, stage, turned, transpose=True)
            factor = [weights[row] for row in rows]
            unit = units[plain][quad % DEEP]
            left = spread((factor[0], factor[2]), (factor[1], factor[3]))
            pltpu.matmul_acc_lhs(unit, left, load_staged_rhs=stage)
            queued.append((grad_sums, ((0, 0), (2, 1), (1, 0), (3, 1)), cols, unit))
            factor = [rewards[col] for col in cols]
            unit = units[turned][quad % DEEP]
            left = spread((factor[0], factor[1]), (factor[2], factor[3]))
            pltpu.matmul_acc_lhs(unit, left, load_staged_rhs=stage)
            queued.append((value_sums, ((0, 0), (1, 1), (2, 0), (3, 1)), rows, unit))
            while len(queued) > 2 * LAG:
                add_next()
        while queued:
            add_next()

    pl.run_scoped(multiply, *[pltpu.ACC(unit)((4 * REWARDS, 2 * BLK), jnp.float32) for unit in (0, 1) for _ in range(DEEP)])

    lines = REWARDS // n_row
    part = row_cells // n_chip

    def put_grad(step, out):
        tiles = out if step == 0 else draft
        for col in range(col_cells):
            here = pl.ds((own_row ^ step) * lines, lines)
            at, line = divmod(col * lines, REWARDS)
            tiles[at, line : line + lines, :] = sum(sums[col, here, :] for sums in grad_sums)
        if step:
            encode(draft, out)

    def put_value(step, out):
        cells = pl.ds((own_chip ^ step) * part, part)
        value = sum(sums[cells] for sums in value_sums)
        if step:
            encode(value, out)
        else:
            out[...] = value

    def put(values, grads):
        for step in range(steps):
            if step < n_chip:
                put_value(step, values[step])
            if step < n_row:
                put_grad(step, grads[step])

    @pl.when(core == 0)
    def _():
        put(keeps, gives)

    @pl.when(core == 1)
    def _():
        put(gives, keeps)


def encode(tiles, out):
    values = [tiles[at] for at in range(out.shape[0] - 1)]
    top = functools.reduce(jnp.maximum, [jnp.abs(value) for value in values])
    power = jnp.ceil(jnp.log2(jnp.maximum(top, 2.0**-100)) * GRAIN)
    out[len(values)] = power.astype(jnp.int32).astype(jnp.int16)
    factor = MOST / jnp.exp2(power / GRAIN)
    for at, value in enumerate(values):
        whole = jnp.clip(jnp.round(value * factor), -MOST, MOST)
        out[at] = whole.astype(jnp.int32).astype(jnp.int16)


def decode(coded, first, count):
    power = coded[first + count].astype(jnp.int32).astype(jnp.float32)
    factor = jnp.exp2(power / GRAIN) / MOST
    return [coded[first + at].astype(jnp.int32).astype(jnp.float32) * factor for at in range(count)]


def pair_kernel(keep, got, out):
    half = keep.shape[0]
    out[:half], out[half:] = by_core(keep[...], got[...])


def total_kernel(n_row, n_chip, *refs):
    parts, (keep, give) = refs[:-2], refs[-2:]
    core = lax.axis_index("col") % 2
    half = keep.shape[0]

    def total(count, side):
        sums = [parts[0][side * half + at] for at in range(half)]
        for part in parts[1:count]:
            arrived = decode(part, side * (half + 1), half)
            sums = [one + other for one, other in zip(sums, arrived)]
        return sums

    @pl.when(core == 0)
    def _():
        cut = half // 2
        for side in range(2):
            sums = total(n_chip, side)
            for at in range(cut):
                keep[side * cut + at], give[side * cut + at] = sums[at], sums[cut + at]

    @pl.when(core == 1)
    def _():
        for side, out in enumerate((give, keep)):
            for at, one in enumerate(total(n_row, side)):
                out[at] = one


def result_kernel(keep, got, value, grad):
    core = lax.axis_index("col") % 2
    lines = grad.shape[0]

    def write(values, grads):
        owned = value.shape[1] // BLK // 2
        for at in range(owned):
            for parity in range(2):
                cell = 2 * at + parity
                value[:, cell * BLK : (cell + 1) * BLK] = values[parity * owned + at]
        for col in range(grad.shape[1] // BLK):
            at, line = divmod(col * lines, REWARDS)
            grad[:, col * BLK : (col + 1) * BLK] = grads[at, line : line + lines, :]

    @pl.when(core == 0)
    def _():
        write(keep, got)

    @pl.when(core == 1)
    def _():
        write(got, keep)


def on_device(n_row, n_col, blocks, slot_rows, slot_cols, counts, reward_table, reward_cols, cotangent):
    n_chip = n_col // 2
    row_cells = n_col * (cotangent.shape[1] // BLK) // 2
    col_cells = reward_table.shape[1] // BLK
    smem = pl.BlockSpec(memory_space=pltpu.SMEM)
    hbm = pl.BlockSpec(memory_space=pltpu.HBM)
    vmem = pl.BlockSpec(memory_space=pltpu.VMEM)
    in_smem = functools.partial(pltpu.with_memory_space_constraint, memory_space=pltpu.SMEM)
    in_hbm = functools.partial(pltpu.with_memory_space_constraint, memory_space=pltpu.HBM)

    steps = max(n_row, n_chip)
    small = pltpu.CompilerParams(vmem_limit_bytes=8 * 2**20)

    def swap(part):
        return lax.ppermute(part, "col", peers(n_col, 1))

    def cross(part, step):
        return lax.ppermute(part, ("row", "col"), crossings(n_row, n_col, step))

    width = 2 * reward_table.shape[0] * reward_table.shape[1] // REWARDS
    loaded = pl.pallas_call(
        load_kernel,
        out_shape=[jax.ShapeDtypeStruct(arg.shape, arg.dtype) for arg in (cotangent, reward_table)],
        in_specs=[hbm] * 2,
        out_specs=[vmem] * 2,
        scratch_shapes=[pltpu.SemaphoreType.DMA((2,))],
        compiler_params=small,
        cost_estimate=pl.CostEstimate(flops=0, bytes_accessed=4 * 2**20, transcendentals=0),
    )(in_hbm(cotangent), in_hbm(reward_table))
    mine, other = pl.pallas_call(
        gather_kernel,
        out_shape=[jax.ShapeDtypeStruct((REWARDS, width), cotangent.dtype)] * 2,
        in_specs=[vmem] * 4,
        out_specs=[vmem] * 2,
        compiler_params=small,
    )(*loaded, swap(cotangent), swap(reward_table))
    mine = [mine] + [cross(mine, step) for step in range(1, steps)]
    side = 2 * BLK
    rows, cols, pick, stored = pl.pallas_call(
        prefetch_kernel,
        out_shape=[
            pltpu.SMEM(slot_rows.shape, slot_rows.dtype),
            pltpu.SMEM(slot_cols.shape, slot_cols.dtype),
            jax.ShapeDtypeStruct((side // (reward_table.shape[0] * n_row) * REWARDS, side), jnp.bfloat16),
            jax.ShapeDtypeStruct((1, 1, blocks.shape[2] - LATE, BLK, BLK), blocks.dtype),
        ],
        in_specs=[vmem] + [hbm] * 4,
        out_specs=[smem] * 2 + [vmem] * 2,
        scratch_shapes=[pltpu.SMEM(reward_cols.shape, jnp.int32), pltpu.SemaphoreType.DMA((4,))],
        compiler_params=pltpu.CompilerParams(vmem_limit_bytes=24 * 2**20),
        cost_estimate=pl.CostEstimate(flops=0, bytes_accessed=2 * blocks.size * 2, transcendentals=0),
    )(mine[0], *map(in_hbm, (slot_rows, slot_cols, reward_cols, blocks)))
    first = pl.pallas_call(
        after_kernel,
        out_shape=jax.ShapeDtypeStruct(mine[-1].shape, mine[-1].dtype),
        in_specs=[vmem] * 2,
        out_specs=vmem,
        compiler_params=small,
    )(mine[-1], pick)
    others = [other] + [swap(part) for part in (*mine[1:-1], first)]

    lines, part = REWARDS // n_row, row_cells // n_chip
    tiles = jax.ShapeDtypeStruct((max(part, col_cells * lines // REWARDS), REWARDS, BLK), jnp.float32)
    coded = jax.ShapeDtypeStruct((tiles.shape[0] + 1, REWARDS, BLK), jnp.int16)
    sums = pl.pallas_call(
        functools.partial(products_kernel, n_row, n_col),
        out_shape=[tiles, *[coded] * (steps - 1)] * 2,
        in_specs=[smem] * 3 + [hbm] + [vmem] * (2 + 2 * steps),
        out_specs=[vmem] * (2 * steps),
        scratch_shapes=[
            pltpu.VMEM((reward_table.shape[0] * n_row, col_cells * BLK), jnp.float32),
            pltpu.VMEM((row_cells + SPARE, REWARDS, BLK), jnp.bfloat16),
            pltpu.VMEM((col_cells + SPARE, REWARDS, BLK), jnp.bfloat16),
            *[pltpu.VMEM((row_cells + SPARE, REWARDS, BLK), jnp.float32)] * SUMS,
            *[pltpu.VMEM((col_cells + SPARE, REWARDS, BLK), jnp.float32)] * SUMS,
            pltpu.VMEM(tiles.shape, jnp.float32),
            pltpu.VMEM((1, 1, LATE, BLK, BLK), blocks.dtype),
            pltpu.SemaphoreType.DMA,
        ],
        compiler_params=pltpu.CompilerParams(vmem_limit_bytes=24 * 2**20),
        cost_estimate=pl.CostEstimate(
            flops=4 * REWARDS * blocks.size, bytes_accessed=4 * blocks.size, transcendentals=0
        ),
    )(counts, *map(in_smem, (rows, cols)), in_hbm(blocks), pick, stored, *mine, *others)
    keeps, gives = sums[:steps], sums[steps:]
    parts = []
    for step in reversed(range(steps)):
        pair = pl.pallas_call(
            pair_kernel,
            out_shape=jax.ShapeDtypeStruct((2 * keeps[step].shape[0], REWARDS, BLK), keeps[step].dtype),
            in_specs=[vmem] * 2,
            out_specs=vmem,
            compiler_params=small,
        )(keeps[step], swap(gives[step]))
        parts.insert(0, cross(pair, step) if step else pair)
    keep, give = pl.pallas_call(
        functools.partial(total_kernel, n_row, n_chip),
        out_shape=[tiles] * 2,
        in_specs=[vmem] * steps,
        out_specs=[vmem] * 2,
        compiler_params=small,
    )(*parts)
    return pl.pallas_call(
        result_kernel,
        out_shape=[
            jax.ShapeDtypeStruct((REWARDS, part * BLK), jnp.float32),
            jax.ShapeDtypeStruct((lines, col_cells * BLK), jnp.float32),
        ],
        in_specs=[vmem] * 2,
        out_specs=[vmem] * 2,
        compiler_params=small,
    )(keep, swap(give))


def solution(mesh):
    placed = (
        P("row", "col", None, None, None),
        P("row", "col", None),
        P("row", "col", None),
        P("row", "col"),
        P("row", "col"),
        P(),
        P(None, ("row", "col")),
    )
    return jax.shard_map(
        functools.partial(on_device, mesh.shape["row"], mesh.shape["col"]),
        mesh=mesh,
        in_specs=placed,
        out_specs=(P(None, ("row", "col")), P("row", "col")),
        check_vma=False,
    )
```

```python
import functools

import jax
import jax.numpy as jnp
from jax import lax
from jax.experimental import pallas as pl
from jax.experimental.pallas import tpu as pltpu
from jax.sharding import PartitionSpec as P

BLK = 128
REWARDS = 16
LATE = 128
PART = 64
SUMS = 1
GRAIN = 128
MOST = 32767.0
SPARE = 8
LAG = 2
DEEP = 4


def peers(size, step):
    return [(here, here ^ step) for here in range(size)]


def far_order(n_row):
    return (2, 1, *range(3, n_row))


def crossings(n_row, n_col, first, second):
    pairs = []
    for row in range(n_row):
        for chip in range(n_col // 2):
            for core, step in enumerate((first, second)):
                if step is not None:
                    pairs.append(
                        (row * n_col + 2 * chip + core, (row ^ step[0]) * n_col + 2 * (chip ^ step[1]) + core)
                    )
    return pairs


def by_core(here, there):
    first = lax.axis_index("col") % 2 == 0
    return jnp.where(first, here, there), jnp.where(first, there, here)


def load_kernel(shard_there, table_there, shard, table, sems):
    copies = [
        pltpu.make_async_copy(shard_there, shard, sems.at[0]),
        pltpu.make_async_copy(table_there, table, sems.at[1]),
    ]
    for copy in copies:
        copy.start()
    for copy in copies:
        copy.wait()


def prefetch_kernel(after, rows_there, cols_there, reward_cols_there, blocks_there, rows, cols, pick, blocks, reward_cols, sems):
    pairs = (
        (reward_cols_there, reward_cols),
        (rows_there, rows),
        (cols_there, cols),
        (blocks_there.at[:, :, pl.ds(0, blocks.shape[2])], blocks),
    )
    copies = [pltpu.make_async_copy(there, here, sems.at[at]) for at, (there, here) in enumerate(pairs)]
    for copy in copies:
        copy.start()
    copies[0].wait()
    own_row = lax.axis_index("row")
    candidates = pick.shape[1] * REWARDS // pick.shape[0]
    group = candidates // lax.axis_size("row")
    lane = lax.broadcasted_iota(jnp.int32, (REWARDS, pick.shape[1]), 1)
    at = lane % candidates
    column = at % group + (own_row ^ (at // group)) * group
    line = lax.broadcasted_iota(jnp.int32, (REWARDS, pick.shape[1]), 0)
    wanted = jnp.zeros(lane.shape, jnp.int32)
    for k in range(REWARDS):
        wanted = jnp.where(line == k, reward_cols[k], wanted)
    hit = column == wanted
    bands = [jnp.where(hit & (lane // candidates == band), 1.0, 0.0) for band in range(pick.shape[1] // candidates)]
    pick[...] = jnp.concatenate(bands, axis=0).astype(jnp.bfloat16)
    for copy in copies[1:]:
        copy.wait()


def gather_kernel(shard, other_shard, cots, cells):
    span, owned, parity = shard.shape[1], cells.shape[0] // 2, lax.axis_index("col") % 2
    cots[:, :span], cots[:, span:] = by_core(shard[...], other_shard[...])
    for at in range(owned):
        lane = pl.ds(pl.multiple_of((2 * at + parity) * BLK, BLK), BLK)
        cells[at], cells[owned + at] = by_core(shard[:, lane], other_shard[:, lane])


def spread(first, second):
    empty = jnp.zeros((2 * REWARDS, BLK), jnp.bfloat16)
    top = jnp.concatenate([jnp.concatenate(first, axis=0), empty], axis=1)
    bottom = jnp.concatenate([empty, jnp.concatenate(second, axis=0)], axis=1)
    return jnp.concatenate([top, bottom], axis=0)


def products_kernel(n_row, n_col, *refs):
    n_chip = n_col // 2
    steps, rounds = max(n_row, n_chip), n_chip // 2 - 1
    counts, slot_rows, slot_cols, blocks_there, pick, blocks, cots, cells = refs[:8]
    mine, others = refs[8 : 8 + rounds], refs[8 + rounds : 8 + 2 * rounds]
    tables = refs[8 + 2 * rounds : 8 + 2 * rounds + n_row]
    refs = refs[8 + 2 * rounds + n_row :]
    keeps, gives = refs[:steps], refs[steps : 2 * steps]
    refs = refs[2 * steps :]
    table, weights, rewards = refs[:3]
    value_sums, grad_sums = refs[3 : 3 + SUMS], refs[3 + SUMS : 3 + 2 * SUMS]
    draft, late, late_sem = refs[3 + 2 * SUMS :]
    own_row, own_col = lax.axis_index("row"), lax.axis_index("col")
    own_chip, core = own_col // 2, own_col % 2
    row_cells, col_cells = weights.shape[0] - SPARE, rewards.shape[0] - SPARE

    early = blocks.shape[2]
    late_copies = [
        pltpu.make_async_copy(
            blocks_there.at[:, :, pl.ds(early + at, PART)], late.at[:, :, pl.ds(at, PART)], late_sem.at[at // PART]
        )
        for at in range(0, LATE, PART)
    ]
    for copy in late_copies:
        copy.start()
    @pl.when(counts[0, 0] >= 0)
    def _():
        for sums in (*value_sums, *grad_sums):
            sums[...] = jnp.zeros_like(sums)

    for spare in range(SPARE):
        weights[row_cells + spare] = jnp.zeros((REWARDS, BLK), jnp.bfloat16)
        rewards[col_cells + spare] = jnp.zeros((REWARDS, BLK), jnp.bfloat16)

    owned = row_cells // n_col
    group = table.shape[0] // n_row

    def take_shards(part, step):
        for half in range(2):
            first = (2 * (own_chip ^ step) + half) * owned
            for at in range(owned):
                lane = pl.multiple_of((half * 2 * owned + 2 * at + core) * BLK, BLK)
                weights[first + at] = part[:, pl.ds(lane, BLK)]

    take_shards(cots, 0)
    for turn in range(rounds):
        take_shards(mine[turn], 2 * turn + 1 + core)
        take_shards(others[turn], 2 * turn + 2 - core)
    weights[pl.ds((own_chip ^ (n_chip - 1)) * 2 * owned, 2 * owned)] = cells[...]
    for step, part in zip((0, *far_order(n_row)), tables):
        table[step * group : (step + 1) * group, :] = part[...].astype(jnp.float32)

    side = 2 * BLK
    bands = side // (group * n_row)

    def pick_rewards(*units):
        for turn in range(col_cells * BLK // (bands * side)):
            unit = turn % 2
            lanes = [pl.ds((turn * bands + band) * side, side) for band in range(bands)]
            tile = jnp.concatenate([table[:, here] for here in lanes], axis=0).astype(jnp.bfloat16)
            pltpu.matmul_push_rhs(tile, 0, unit)
            pltpu.matmul_acc_lhs(units[unit], pick[...], load_staged_rhs=0)
            product = pltpu.matmul_pop(units[unit]).astype(jnp.bfloat16)
            for cell in range(2 * bands):
                band, half = divmod(cell, 2)
                rewards[turn * 2 * bands + cell] = product[
                    band * REWARDS : (band + 1) * REWARDS, half * BLK : (half + 1) * BLK
                ]

    pl.run_scoped(pick_rewards, *[pltpu.ACC(unit)((bands * REWARDS, side), jnp.float32) for unit in (0, 1)])

    live_count = counts[0, 0]

    def multiply(*held):
        units = (held[:DEEP], held[DEEP:])
        queued = []

        def add_next():
            totals, order, cells, unit = queued.pop(0)
            product = pltpu.matmul_pop(unit)
            for piece, (at, side) in enumerate(order):
                part = product[piece * REWARDS : (piece + 1) * REWARDS, side * BLK : (side + 1) * BLK]
                totals[at % SUMS][cells[at]] += part

        for quad in range((early + LATE) // 4):
            start = quad * 4
            if start >= early and (start - early) % PART == 0:
                late_copies[(start - early) // PART].wait()
            rows, cols = [], []
            for at in range(4):
                live = start + at < live_count
                rows.append(jnp.where(live, slot_rows[0, 0, start + at] // 2, row_cells + (start + at) % SPARE))
                cols.append(jnp.where(live, slot_cols[0, 0, start + at], col_cells + (start + at) % SPARE))
            held_in, first = (blocks, start) if start < early else (late, start - early)
            stored = [held_in[0, 0, first + at] for at in range(4)]
            tile = jnp.concatenate(
                [jnp.concatenate(stored[:2], axis=0), jnp.concatenate(stored[2:], axis=0)], axis=1
            )
            plain, turned, stage = quad % 2, 1 - quad % 2, quad % 2
            pltpu.matmul_push_rhs(tile, stage, plain)
            pltpu.matmul_push_rhs(tile, stage, turned, transpose=True)
            factor = [weights[row] for row in rows]
            unit = units[plain][quad % DEEP]
            left = spread((factor[0], factor[2]), (factor[1], factor[3]))
            pltpu.matmul_acc_lhs(unit, left, load_staged_rhs=stage)
            queued.append((grad_sums, ((0, 0), (2, 1), (1, 0), (3, 1)), cols, unit))
            factor = [rewards[col] for col in cols]
            unit = units[turned][quad % DEEP]
            left = spread((factor[0], factor[1]), (factor[2], factor[3]))
            pltpu.matmul_acc_lhs(unit, left, load_staged_rhs=stage)
            queued.append((value_sums, ((0, 0), (1, 1), (2, 0), (3, 1)), rows, unit))
            while len(queued) > 2 * LAG:
                add_next()
        while queued:
            add_next()

    pl.run_scoped(multiply, *[pltpu.ACC(unit)((4 * REWARDS, 2 * BLK), jnp.float32) for unit in (0, 1) for _ in range(DEEP)])

    lines = REWARDS // n_row
    part = row_cells // n_chip

    def put_grad(step, out):
        tiles = out if step == 0 else draft
        for col in range(col_cells):
            here = pl.ds((own_row ^ step) * lines, lines)
            at, line = divmod(col * lines, REWARDS)
            tiles[at, line : line + lines, :] = sum(sums[col, here, :] for sums in grad_sums)
        if step:
            encode(draft, out)

    def put_value(step, out):
        cells = pl.ds((own_chip ^ step) * part, part)
        value = sum(sums[cells] for sums in value_sums)
        if step:
            encode(value, out)
        else:
            out[...] = value

    def put(values, grads):
        for step in range(steps):
            if step < n_chip:
                put_value(step, values[step])
            if step < n_row:
                put_grad(step, grads[step])

    @pl.when(core == 0)
    def _():
        put(keeps, gives)

    @pl.when(core == 1)
    def _():
        put(gives, keeps)


def encode(tiles, out):
    values = [tiles[at] for at in range(out.shape[0] - 1)]
    top = functools.reduce(jnp.maximum, [jnp.abs(value) for value in values])
    power = jnp.ceil(jnp.log2(jnp.maximum(top, 2.0**-100)) * GRAIN)
    out[len(values)] = power.astype(jnp.int32).astype(jnp.int16)
    factor = MOST / jnp.exp2(power / GRAIN)
    for at, value in enumerate(values):
        whole = jnp.clip(jnp.round(value * factor), -MOST, MOST)
        out[at] = whole.astype(jnp.int32).astype(jnp.int16)


def decode(coded, first, count):
    power = coded[first + count].astype(jnp.int32).astype(jnp.float32)
    factor = jnp.exp2(power / GRAIN) / MOST
    return [coded[first + at].astype(jnp.int32).astype(jnp.float32) * factor for at in range(count)]


def pair_kernel(keep, got, out):
    half = keep.shape[0]
    out[:half], out[half:] = by_core(keep[...], got[...])


def total_kernel(n_row, n_chip, *refs):
    parts, (keep, give) = refs[:-2], refs[-2:]
    core = lax.axis_index("col") % 2
    half = keep.shape[0]

    def total(count, side):
        sums = [parts[0][side * half + at] for at in range(half)]
        for part in parts[1:count]:
            arrived = decode(part, side * (half + 1), half)
            sums = [one + other for one, other in zip(sums, arrived)]
        return sums

    @pl.when(core == 0)
    def _():
        cut = half // 2
        for side in range(2):
            sums = total(n_chip, side)
            for at in range(cut):
                keep[side * cut + at], give[side * cut + at] = sums[at], sums[cut + at]

    @pl.when(core == 1)
    def _():
        for side, out in enumerate((give, keep)):
            for at, one in enumerate(total(n_row, side)):
                out[at] = one


def result_kernel(keep, got, value, grad):
    core = lax.axis_index("col") % 2
    lines = grad.shape[0]

    def write(values, grads):
        owned = value.shape[1] // BLK // 2
        for at in range(owned):
            for parity in range(2):
                cell = 2 * at + parity
                value[:, cell * BLK : (cell + 1) * BLK] = values[parity * owned + at]
        for col in range(grad.shape[1] // BLK):
            at, line = divmod(col * lines, REWARDS)
            grad[:, col * BLK : (col + 1) * BLK] = grads[at, line : line + lines, :]

    @pl.when(core == 0)
    def _():
        write(keep, got)

    @pl.when(core == 1)
    def _():
        write(got, keep)


def on_device(n_row, n_col, blocks, slot_rows, slot_cols, counts, reward_table, reward_cols, cotangent):
    n_chip = n_col // 2
    row_cells = n_col * (cotangent.shape[1] // BLK) // 2
    col_cells = reward_table.shape[1] // BLK
    smem = pl.BlockSpec(memory_space=pltpu.SMEM)
    hbm = pl.BlockSpec(memory_space=pltpu.HBM)
    vmem = pl.BlockSpec(memory_space=pltpu.VMEM)
    in_smem = functools.partial(pltpu.with_memory_space_constraint, memory_space=pltpu.SMEM)
    in_hbm = functools.partial(pltpu.with_memory_space_constraint, memory_space=pltpu.HBM)

    steps = max(n_row, n_chip)
    small = pltpu.CompilerParams(vmem_limit_bytes=8 * 2**20)

    def swap(part):
        return lax.ppermute(part, "col", peers(n_col, 1))

    def cross(part, first, second):
        return lax.ppermute(part, ("row", "col"), crossings(n_row, n_col, first, second))

    loaded = pl.pallas_call(
        load_kernel,
        out_shape=[jax.ShapeDtypeStruct(arg.shape, arg.dtype) for arg in (cotangent, reward_table)],
        in_specs=[hbm] * 2,
        out_specs=[vmem] * 2,
        scratch_shapes=[pltpu.SemaphoreType.DMA((2,))],
        compiler_params=small,
        cost_estimate=pl.CostEstimate(flops=0, bytes_accessed=4 * 2**20, transcendentals=0),
    )(in_hbm(cotangent), in_hbm(reward_table))
    cots, cells = pl.pallas_call(
        gather_kernel,
        out_shape=[
            jax.ShapeDtypeStruct((REWARDS, 2 * cotangent.shape[1]), cotangent.dtype),
            jax.ShapeDtypeStruct((row_cells // n_chip, REWARDS, BLK), cotangent.dtype),
        ],
        in_specs=[vmem] * 2,
        out_specs=[vmem] * 2,
        compiler_params=small,
    )(loaded[0], swap(cotangent))
    mine = [cross(cots, (0, 2 * turn + 1), (0, 2 * turn + 2)) for turn in range(n_chip // 2 - 1)]
    others = [swap(part) for part in mine]
    tables = [loaded[1]] + [lax.ppermute(reward_table, "row", peers(n_row, step)) for step in far_order(n_row)]
    opposite = lax.ppermute(cells, "col", peers(n_col, 2 * (n_chip - 1)))
    side = 2 * BLK
    rows, cols, pick, stored = pl.pallas_call(
        prefetch_kernel,
        out_shape=[
            pltpu.SMEM(slot_rows.shape, slot_rows.dtype),
            pltpu.SMEM(slot_cols.shape, slot_cols.dtype),
            jax.ShapeDtypeStruct((side // (reward_table.shape[0] * n_row) * REWARDS, side), jnp.bfloat16),
            jax.ShapeDtypeStruct((1, 1, blocks.shape[2] - LATE, BLK, BLK), blocks.dtype),
        ],
        in_specs=[vmem] + [hbm] * 4,
        out_specs=[smem] * 2 + [vmem] * 2,
        scratch_shapes=[pltpu.SMEM(reward_cols.shape, jnp.int32), pltpu.SemaphoreType.DMA((4,))],
        compiler_params=pltpu.CompilerParams(vmem_limit_bytes=24 * 2**20),
        cost_estimate=pl.CostEstimate(flops=0, bytes_accessed=2 * blocks.size * 2, transcendentals=0),
    )(mine[0], *map(in_hbm, (slot_rows, slot_cols, reward_cols, blocks)))

    lines, part = REWARDS // n_row, row_cells // n_chip
    tiles = jax.ShapeDtypeStruct((max(part, col_cells * lines // REWARDS), REWARDS, BLK), jnp.float32)
    coded = jax.ShapeDtypeStruct((tiles.shape[0] + 1, REWARDS, BLK), jnp.int16)
    sums = pl.pallas_call(
        functools.partial(products_kernel, n_row, n_col),
        out_shape=[tiles, *[coded] * (steps - 1)] * 2,
        in_specs=[smem] * 3 + [hbm] + [vmem] * (4 + 2 * len(mine) + n_row),
        out_specs=[vmem] * (2 * steps),
        scratch_shapes=[
            pltpu.VMEM((reward_table.shape[0] * n_row, col_cells * BLK), jnp.float32),
            pltpu.VMEM((row_cells + SPARE, REWARDS, BLK), jnp.bfloat16),
            pltpu.VMEM((col_cells + SPARE, REWARDS, BLK), jnp.bfloat16),
            *[pltpu.VMEM((row_cells + SPARE, REWARDS, BLK), jnp.float32)] * SUMS,
            *[pltpu.VMEM((col_cells + SPARE, REWARDS, BLK), jnp.float32)] * SUMS,
            pltpu.VMEM(tiles.shape, jnp.float32),
            pltpu.VMEM((1, 1, LATE, BLK, BLK), blocks.dtype),
            pltpu.SemaphoreType.DMA((LATE // PART,)),
        ],
        compiler_params=pltpu.CompilerParams(vmem_limit_bytes=24 * 2**20),
        cost_estimate=pl.CostEstimate(
            flops=4 * REWARDS * blocks.size, bytes_accessed=4 * blocks.size, transcendentals=0
        ),
    )(counts, *map(in_smem, (rows, cols)), in_hbm(blocks), pick, stored, cots, opposite, *mine, *others, *tables)
    keeps, gives = sums[:steps], sums[steps:]
    parts = []
    for step in reversed(range(steps)):
        pair = pl.pallas_call(
            pair_kernel,
            out_shape=jax.ShapeDtypeStruct((2 * keeps[step].shape[0], REWARDS, BLK), keeps[step].dtype),
            in_specs=[vmem] * 2,
            out_specs=vmem,
            compiler_params=small,
        )(keeps[step], swap(gives[step]))
        parts.insert(0, cross(pair, (0, step) if step < n_chip else None, (step, 0) if step < n_row else None) if step else pair)
    keep, give = pl.pallas_call(
        functools.partial(total_kernel, n_row, n_chip),
        out_shape=[tiles] * 2,
        in_specs=[vmem] * steps,
        out_specs=[vmem] * 2,
        compiler_params=small,
    )(*parts)
    return pl.pallas_call(
        result_kernel,
        out_shape=[
            jax.ShapeDtypeStruct((REWARDS, part * BLK), jnp.float32),
            jax.ShapeDtypeStruct((lines, col_cells * BLK), jnp.float32),
        ],
        in_specs=[vmem] * 2,
        out_specs=[vmem] * 2,
        compiler_params=small,
    )(keep, swap(give))


def solution(mesh):
    placed = (
        P("row", "col", None, None, None),
        P("row", "col", None),
        P("row", "col", None),
        P("row", "col"),
        P("row", "col"),
        P(),
        P(None, ("row", "col")),
    )
    return jax.shard_map(
        functools.partial(on_device, mesh.shape["row"], mesh.shape["col"]),
        mesh=mesh,
        in_specs=placed,
        out_specs=(P(None, ("row", "col")), P("row", "col")),
        check_vma=False,
    )
```

```python
import functools

import jax
import jax.numpy as jnp
from jax import lax
from jax.experimental import pallas as pl
from jax.experimental.pallas import tpu as pltpu
from jax.sharding import PartitionSpec as P

BLK = 128
REWARDS = 16
LATE = 160
PART = 32
SUMS = 1
GRAIN = 128
MOST = 32767.0
SPARE = 8
LAG = 2
DEEP = 4


def peers(size, step):
    return [(here, here ^ step) for here in range(size)]


def far_order(n_row):
    return (2, 1, *range(3, n_row))


def crossings(n_row, n_col, first, second):
    pairs = []
    for row in range(n_row):
        for chip in range(n_col // 2):
            for core, step in enumerate((first, second)):
                if step is not None:
                    pairs.append(
                        (row * n_col + 2 * chip + core, (row ^ step[0]) * n_col + 2 * (chip ^ step[1]) + core)
                    )
    return pairs


def by_core(here, there):
    first = lax.axis_index("col") % 2 == 0
    return jnp.where(first, here, there), jnp.where(first, there, here)


def load_kernel(shard_there, table_there, shard, table, sems):
    copies = [
        pltpu.make_async_copy(shard_there, shard, sems.at[0]),
        pltpu.make_async_copy(table_there, table, sems.at[1]),
    ]
    for copy in copies:
        copy.start()
    for copy in copies:
        copy.wait()


def prefetch_kernel(after, rows_there, cols_there, reward_cols_there, blocks_there, rows, cols, pick, blocks, reward_cols, sems):
    pairs = (
        (reward_cols_there, reward_cols),
        (rows_there, rows),
        (cols_there, cols),
        (blocks_there.at[:, :, pl.ds(0, blocks.shape[2])], blocks),
    )
    copies = [pltpu.make_async_copy(there, here, sems.at[at]) for at, (there, here) in enumerate(pairs)]
    for copy in copies:
        copy.start()
    copies[0].wait()
    own_row = lax.axis_index("row")
    candidates = pick.shape[1] * REWARDS // pick.shape[0]
    group = candidates // lax.axis_size("row")
    lane = lax.broadcasted_iota(jnp.int32, (REWARDS, pick.shape[1]), 1)
    at = lane % candidates
    column = at % group + (own_row ^ (at // group)) * group
    line = lax.broadcasted_iota(jnp.int32, (REWARDS, pick.shape[1]), 0)
    wanted = jnp.zeros(lane.shape, jnp.int32)
    for k in range(REWARDS):
        wanted = jnp.where(line == k, reward_cols[k], wanted)
    hit = column == wanted
    bands = [jnp.where(hit & (lane // candidates == band), 1.0, 0.0) for band in range(pick.shape[1] // candidates)]
    pick[...] = jnp.concatenate(bands, axis=0).astype(jnp.bfloat16)
    for copy in copies[1:]:
        copy.wait()


def gather_kernel(shard, other_shard, cots, cells):
    span, owned, parity = shard.shape[1], cells.shape[0] // 2, lax.axis_index("col") % 2
    cots[:, :span], cots[:, span:] = by_core(shard[...], other_shard[...])
    for at in range(owned):
        lane = pl.ds(pl.multiple_of((2 * at + parity) * BLK, BLK), BLK)
        cells[at], cells[owned + at] = by_core(shard[:, lane], other_shard[:, lane])


def spread(first, second):
    empty = jnp.zeros((2 * REWARDS, BLK), jnp.bfloat16)
    top = jnp.concatenate([jnp.concatenate(first, axis=0), empty], axis=1)
    bottom = jnp.concatenate([empty, jnp.concatenate(second, axis=0)], axis=1)
    return jnp.concatenate([top, bottom], axis=0)


def products_kernel(n_row, n_col, *refs):
    n_chip = n_col // 2
    steps, rounds = max(n_row, n_chip), n_chip // 2 - 1
    counts, slot_rows, slot_cols, blocks_there, pick, blocks, cots, cells = refs[:8]
    mine, others = refs[8 : 8 + rounds], refs[8 + rounds : 8 + 2 * rounds]
    tables = refs[8 + 2 * rounds : 8 + 2 * rounds + n_row]
    refs = refs[8 + 2 * rounds + n_row :]
    keeps, gives = refs[:steps], refs[steps : 2 * steps]
    refs = refs[2 * steps :]
    table, weights, rewards = refs[:3]
    value_sums, grad_sums = refs[3 : 3 + SUMS], refs[3 + SUMS : 3 + 2 * SUMS]
    draft, late, late_sem = refs[3 + 2 * SUMS :]
    own_row, own_col = lax.axis_index("row"), lax.axis_index("col")
    own_chip, core = own_col // 2, own_col % 2
    row_cells, col_cells = weights.shape[0] - SPARE, rewards.shape[0] - SPARE

    early = blocks.shape[2]
    late_copies = [
        pltpu.make_async_copy(
            blocks_there.at[:, :, pl.ds(early + at, PART)], late.at[:, :, pl.ds(at, PART)], late_sem.at[at // PART]
        )
        for at in range(0, LATE, PART)
    ]
    for copy in late_copies:
        copy.start()
    @pl.when(counts[0, 0] >= 0)
    def _():
        for sums in (*value_sums, *grad_sums):
            sums[...] = jnp.zeros_like(sums)

    for spare in range(SPARE):
        weights[row_cells + spare] = jnp.zeros((REWARDS, BLK), jnp.bfloat16)
        rewards[col_cells + spare] = jnp.zeros((REWARDS, BLK), jnp.bfloat16)

    owned = row_cells // n_col
    group = table.shape[0] // n_row

    def take_shards(part, step):
        for half in range(2):
            first = (2 * (own_chip ^ step) + half) * owned
            for at in range(owned):
                lane = pl.multiple_of((half * 2 * owned + 2 * at + core) * BLK, BLK)
                weights[first + at] = part[:, pl.ds(lane, BLK)]

    take_shards(cots, 0)
    for turn in range(rounds):
        take_shards(mine[turn], 2 * turn + 1 + core)
        take_shards(others[turn], 2 * turn + 2 - core)
    weights[pl.ds((own_chip ^ (n_chip - 1)) * 2 * owned, 2 * owned)] = cells[...]
    for step, part in zip((0, *far_order(n_row)), tables):
        table[step * group : (step + 1) * group, :] = part[...].astype(jnp.float32)

    side = 2 * BLK
    bands = side // (group * n_row)

    def pick_rewards(*units):
        for turn in range(col_cells * BLK // (bands * side)):
            unit = turn % 2
            lanes = [pl.ds((turn * bands + band) * side, side) for band in range(bands)]
            tile = jnp.concatenate([table[:, here] for here in lanes], axis=0).astype(jnp.bfloat16)
            pltpu.matmul_push_rhs(tile, 0, unit)
            pltpu.matmul_acc_lhs(units[unit], pick[...], load_staged_rhs=0)
            product = pltpu.matmul_pop(units[unit]).astype(jnp.bfloat16)
            for cell in range(2 * bands):
                band, half = divmod(cell, 2)
                rewards[turn * 2 * bands + cell] = product[
                    band * REWARDS : (band + 1) * REWARDS, half * BLK : (half + 1) * BLK
                ]

    pl.run_scoped(pick_rewards, *[pltpu.ACC(unit)((bands * REWARDS, side), jnp.float32) for unit in (0, 1)])

    live_count = counts[0, 0]

    def multiply(*held):
        units = (held[:DEEP], held[DEEP:])
        queued = []

        def add_next():
            totals, order, cells, unit = queued.pop(0)
            product = pltpu.matmul_pop(unit)
            for piece, (at, side) in enumerate(order):
                part = product[piece * REWARDS : (piece + 1) * REWARDS, side * BLK : (side + 1) * BLK]
                totals[at % SUMS][cells[at]] += part

        for quad in range((early + LATE) // 4):
            start = quad * 4
            if start >= early and (start - early) % PART == 0:
                late_copies[(start - early) // PART].wait()
            rows, cols = [], []
            for at in range(4):
                live = start + at < live_count
                rows.append(jnp.where(live, slot_rows[0, 0, start + at] // 2, row_cells + (start + at) % SPARE))
                cols.append(jnp.where(live, slot_cols[0, 0, start + at], col_cells + (start + at) % SPARE))
            held_in, first = (blocks, start) if start < early else (late, start - early)
            stored = [held_in[0, 0, first + at] for at in range(4)]
            tile = jnp.concatenate(
                [jnp.concatenate(stored[:2], axis=0), jnp.concatenate(stored[2:], axis=0)], axis=1
            )
            plain, turned, stage = quad % 2, 1 - quad % 2, quad % 2
            pltpu.matmul_push_rhs(tile, stage, plain)
            pltpu.matmul_push_rhs(tile, stage, turned, transpose=True)
            factor = [weights[row] for row in rows]
            unit = units[plain][quad % DEEP]
            left = spread((factor[0], factor[2]), (factor[1], factor[3]))
            pltpu.matmul_acc_lhs(unit, left, load_staged_rhs=stage)
            queued.append((grad_sums, ((0, 0), (2, 1), (1, 0), (3, 1)), cols, unit))
            factor = [rewards[col] for col in cols]
            unit = units[turned][quad % DEEP]
            left = spread((factor[0], factor[1]), (factor[2], factor[3]))
            pltpu.matmul_acc_lhs(unit, left, load_staged_rhs=stage)
            queued.append((value_sums, ((0, 0), (1, 1), (2, 0), (3, 1)), rows, unit))
            while len(queued) > 2 * LAG:
                add_next()
        while queued:
            add_next()

    pl.run_scoped(multiply, *[pltpu.ACC(unit)((4 * REWARDS, 2 * BLK), jnp.float32) for unit in (0, 1) for _ in range(DEEP)])

    lines = REWARDS // n_row
    part = row_cells // n_chip

    def put_grad(step, out):
        tiles = out if step == 0 else draft
        for col in range(col_cells):
            here = pl.ds((own_row ^ step) * lines, lines)
            at, line = divmod(col * lines, REWARDS)
            tiles[at, line : line + lines, :] = sum(sums[col, here, :] for sums in grad_sums)
        if step:
            encode(draft, out)

    def put_value(step, out):
        cells = pl.ds((own_chip ^ step) * part, part)
        value = sum(sums[cells] for sums in value_sums)
        if step:
            encode(value, out)
        else:
            out[...] = value

    def put(values, grads):
        for step in range(steps):
            if step < n_chip:
                put_value(step, values[step])
            if step < n_row:
                put_grad(step, grads[step])

    @pl.when(core == 0)
    def _():
        put(keeps, gives)

    @pl.when(core == 1)
    def _():
        put(gives, keeps)


def encode(tiles, out):
    values = [tiles[at] for at in range(out.shape[0] - 1)]
    top = functools.reduce(jnp.maximum, [jnp.abs(value) for value in values])
    power = jnp.ceil(jnp.log2(jnp.maximum(top, 2.0**-100)) * GRAIN)
    out[len(values)] = power.astype(jnp.int32).astype(jnp.int16)
    factor = MOST / jnp.exp2(power / GRAIN)
    for at, value in enumerate(values):
        whole = jnp.clip(jnp.round(value * factor), -MOST, MOST)
        out[at] = whole.astype(jnp.int32).astype(jnp.int16)


def decode(coded, first, count):
    power = coded[first + count].astype(jnp.int32).astype(jnp.float32)
    factor = jnp.exp2(power / GRAIN) / MOST
    return [coded[first + at].astype(jnp.int32).astype(jnp.float32) * factor for at in range(count)]


def pair_kernel(keep, got, out):
    half = keep.shape[0]
    out[:half], out[half:] = by_core(keep[...], got[...])


def total_kernel(n_row, n_chip, *refs):
    parts, (keep, give) = refs[:-2], refs[-2:]
    core = lax.axis_index("col") % 2
    half = keep.shape[0]

    def total(count, side):
        sums = [parts[0][side * half + at] for at in range(half)]
        for part in parts[1:count]:
            arrived = decode(part, side * (half + 1), half)
            sums = [one + other for one, other in zip(sums, arrived)]
        return sums

    @pl.when(core == 0)
    def _():
        cut = half // 2
        for side in range(2):
            sums = total(n_chip, side)
            for at in range(cut):
                keep[side * cut + at], give[side * cut + at] = sums[at], sums[cut + at]

    @pl.when(core == 1)
    def _():
        for side, out in enumerate((give, keep)):
            for at, one in enumerate(total(n_row, side)):
                out[at] = one


def result_kernel(keep, got, value, grad):
    core = lax.axis_index("col") % 2
    lines = grad.shape[0]

    def write(values, grads):
        owned = value.shape[1] // BLK // 2
        for at in range(owned):
            for parity in range(2):
                cell = 2 * at + parity
                value[:, cell * BLK : (cell + 1) * BLK] = values[parity * owned + at]
        for col in range(grad.shape[1] // BLK):
            at, line = divmod(col * lines, REWARDS)
            grad[:, col * BLK : (col + 1) * BLK] = grads[at, line : line + lines, :]

    @pl.when(core == 0)
    def _():
        write(keep, got)

    @pl.when(core == 1)
    def _():
        write(got, keep)


def on_device(n_row, n_col, blocks, slot_rows, slot_cols, counts, reward_table, reward_cols, cotangent):
    n_chip = n_col // 2
    row_cells = n_col * (cotangent.shape[1] // BLK) // 2
    col_cells = reward_table.shape[1] // BLK
    smem = pl.BlockSpec(memory_space=pltpu.SMEM)
    hbm = pl.BlockSpec(memory_space=pltpu.HBM)
    vmem = pl.BlockSpec(memory_space=pltpu.VMEM)
    in_smem = functools.partial(pltpu.with_memory_space_constraint, memory_space=pltpu.SMEM)
    in_hbm = functools.partial(pltpu.with_memory_space_constraint, memory_space=pltpu.HBM)

    steps = max(n_row, n_chip)
    small = pltpu.CompilerParams(vmem_limit_bytes=8 * 2**20)

    def swap(part):
        return lax.ppermute(part, "col", peers(n_col, 1))

    def cross(part, first, second):
        return lax.ppermute(part, ("row", "col"), crossings(n_row, n_col, first, second))

    loaded = pl.pallas_call(
        load_kernel,
        out_shape=[jax.ShapeDtypeStruct(arg.shape, arg.dtype) for arg in (cotangent, reward_table)],
        in_specs=[hbm] * 2,
        out_specs=[vmem] * 2,
        scratch_shapes=[pltpu.SemaphoreType.DMA((2,))],
        compiler_params=small,
        cost_estimate=pl.CostEstimate(flops=0, bytes_accessed=4 * 2**20, transcendentals=0),
    )(in_hbm(cotangent), in_hbm(reward_table))
    cots, cells = pl.pallas_call(
        gather_kernel,
        out_shape=[
            jax.ShapeDtypeStruct((REWARDS, 2 * cotangent.shape[1]), cotangent.dtype),
            jax.ShapeDtypeStruct((row_cells // n_chip, REWARDS, BLK), cotangent.dtype),
        ],
        in_specs=[vmem] * 2,
        out_specs=[vmem] * 2,
        compiler_params=small,
    )(loaded[0], swap(cotangent))
    mine = [cross(cots, (0, 2 * turn + 1), (0, 2 * turn + 2)) for turn in range(n_chip // 2 - 1)]
    others = [swap(part) for part in mine]
    tables = [loaded[1]] + [lax.ppermute(reward_table, "row", peers(n_row, step)) for step in far_order(n_row)]
    opposite = lax.ppermute(cells, "col", peers(n_col, 2 * (n_chip - 1)))
    side = 2 * BLK
    rows, cols, pick, stored = pl.pallas_call(
        prefetch_kernel,
        out_shape=[
            pltpu.SMEM(slot_rows.shape, slot_rows.dtype),
            pltpu.SMEM(slot_cols.shape, slot_cols.dtype),
            jax.ShapeDtypeStruct((side // (reward_table.shape[0] * n_row) * REWARDS, side), jnp.bfloat16),
            jax.ShapeDtypeStruct((1, 1, blocks.shape[2] - LATE, BLK, BLK), blocks.dtype),
        ],
        in_specs=[vmem] + [hbm] * 4,
        out_specs=[smem] * 2 + [vmem] * 2,
        scratch_shapes=[pltpu.SMEM(reward_cols.shape, jnp.int32), pltpu.SemaphoreType.DMA((4,))],
        compiler_params=pltpu.CompilerParams(vmem_limit_bytes=24 * 2**20),
        cost_estimate=pl.CostEstimate(flops=0, bytes_accessed=2 * blocks.size * 2, transcendentals=0),
    )(mine[0], *map(in_hbm, (slot_rows, slot_cols, reward_cols, blocks)))

    lines, part = REWARDS // n_row, row_cells // n_chip
    tiles = jax.ShapeDtypeStruct((max(part, col_cells * lines // REWARDS), REWARDS, BLK), jnp.float32)
    coded = jax.ShapeDtypeStruct((tiles.shape[0] + 1, REWARDS, BLK), jnp.int16)
    sums = pl.pallas_call(
        functools.partial(products_kernel, n_row, n_col),
        out_shape=[tiles, *[coded] * (steps - 1)] * 2,
        in_specs=[smem] * 3 + [hbm] + [vmem] * (4 + 2 * len(mine) + n_row),
        out_specs=[vmem] * (2 * steps),
        scratch_shapes=[
            pltpu.VMEM((reward_table.shape[0] * n_row, col_cells * BLK), jnp.float32),
            pltpu.VMEM((row_cells + SPARE, REWARDS, BLK), jnp.bfloat16),
            pltpu.VMEM((col_cells + SPARE, REWARDS, BLK), jnp.bfloat16),
            *[pltpu.VMEM((row_cells + SPARE, REWARDS, BLK), jnp.float32)] * SUMS,
            *[pltpu.VMEM((col_cells + SPARE, REWARDS, BLK), jnp.float32)] * SUMS,
            pltpu.VMEM(tiles.shape, jnp.float32),
            pltpu.VMEM((1, 1, LATE, BLK, BLK), blocks.dtype),
            pltpu.SemaphoreType.DMA((LATE // PART,)),
        ],
        compiler_params=pltpu.CompilerParams(vmem_limit_bytes=24 * 2**20),
        cost_estimate=pl.CostEstimate(
            flops=4 * REWARDS * blocks.size, bytes_accessed=4 * blocks.size, transcendentals=0
        ),
    )(counts, *map(in_smem, (rows, cols)), in_hbm(blocks), pick, stored, cots, opposite, *mine, *others, *tables)
    keeps, gives = sums[:steps], sums[steps:]
    parts = []
    for step in reversed(range(steps)):
        pair = pl.pallas_call(
            pair_kernel,
            out_shape=jax.ShapeDtypeStruct((2 * keeps[step].shape[0], REWARDS, BLK), keeps[step].dtype),
            in_specs=[vmem] * 2,
            out_specs=vmem,
            compiler_params=small,
        )(keeps[step], swap(gives[step]))
        parts.insert(0, cross(pair, (0, step) if step < n_chip else None, (step, 0) if step < n_row else None) if step else pair)
    keep, give = pl.pallas_call(
        functools.partial(total_kernel, n_row, n_chip),
        out_shape=[tiles] * 2,
        in_specs=[vmem] * steps,
        out_specs=[vmem] * 2,
        compiler_params=small,
    )(*parts)
    return pl.pallas_call(
        result_kernel,
        out_shape=[
            jax.ShapeDtypeStruct((REWARDS, part * BLK), jnp.float32),
            jax.ShapeDtypeStruct((lines, col_cells * BLK), jnp.float32),
        ],
        in_specs=[vmem] * 2,
        out_specs=[vmem] * 2,
        compiler_params=small,
    )(keep, swap(give))


def solution(mesh):
    placed = (
        P("row", "col", None, None, None),
        P("row", "col", None),
        P("row", "col", None),
        P("row", "col"),
        P("row", "col"),
        P(),
        P(None, ("row", "col")),
    )
    return jax.shard_map(
        functools.partial(on_device, mesh.shape["row"], mesh.shape["col"]),
        mesh=mesh,
        in_specs=placed,
        out_specs=(P(None, ("row", "col")), P("row", "col")),
        check_vma=False,
    )
```
